32 devices in a mesh: row: 4 (over y, x), col: 4 (over z), depth: 2 (over core).
Axes of the slice: x: 2, y: 2, z: 4, core: 2. Of those that a mesh axis runs over, the one named last changes fastest.
Arguments:
- matrix_tiles: bfloat16 [64, 3, 512, 512], P(('row', 'col', 'depth')), may hold values from 0.00029945374 to 0.29882812
- pattern: int32 [64, 3], replicated, may hold values from 0 to 63, as said below
Outputs:
- inflated: bfloat16 [64, 9, 512, 512], P(('row', 'col', 'depth'))
The draws below stay inside these ranges and needn't reach their ends.
Inputs may be any that keep to these rules, and one draw needn't show every extreme that they name: `pattern`: row i lists 3 different block columns: i itself first, then one at distance exactly 2 from i, then others at distance 1 to 2 from i, all inside the matrix.
All inputs are finite; a program needn't handle non-finite values.
Results may differ from the reference program's by a relative error of at most 0.0071.
Values may be sent and summed in bfloat16 or wider, within the bound.
No kernel may reach another device: no remote copies, remote signals or barrier semaphores. Data moves between devices by JAX's collectives and lax.ppermute only.
A program may use at most 128 MiB of HBM per device.

```python
import math
import jax
import jax.numpy as jnp
from jax import lax

B = 512
S = 3
W = 2
NB = 64


def draw_pattern(key, part):
    row_ids = jnp.arange(NB, dtype=jnp.int32)
    side_key, score_key = jax.random.split(key)
    far_side = jax.random.randint(side_key, (NB,), 0, 2).astype(jnp.int32) * 2 - 1
    far_side = jnp.where(row_ids - W < 0, 1, far_side)
    far_side = jnp.where(row_ids + W > NB - 1, -1, far_side)
    distant_offset = far_side * W
    candidates = jnp.concatenate([jnp.arange(-W, 0, dtype=jnp.int32), jnp.arange(1, W + 1, dtype=jnp.int32)])
    reached = row_ids[:, None] + candidates[None, :]
    usable = (reached >= 0) & (reached < NB) & (candidates[None, :] != distant_offset[:, None])
    scores = jax.random.randint(score_key, (NB, 2 * W), 0, 1 << 20).astype(jnp.int32) * (2 * W) + jnp.arange(2 * W, dtype=jnp.int32)[None, :]
    scores = jnp.where(usable, scores, -1)
    chosen = lax.top_k(scores, S - 2)[1]
    nearby = jnp.take_along_axis(reached, chosen, axis=1)
    return jnp.concatenate([row_ids[:, None], (row_ids + distant_offset)[:, None], nearby], axis=1).astype(jnp.int32)


def block_levels(own_key, extent, cuts, smallest, high):
    level, own = 1.0, jax.random.fold_in(own_key, 6)
    for axis_at, blocks in cuts:
        heights = jnp.exp(jax.random.uniform(jax.random.fold_in(own, axis_at), (blocks,), jnp.float32, smallest / len(cuts), high / len(cuts)))
        level = level * jnp.repeat(heights, extent[axis_at] // blocks).reshape([-1 if axis == axis_at else 1 for axis in range(len(extent))])
    return level


def setup_inputs(seed: int = 0) -> dict:
    arg_keys = jax.random.split(jax.random.key(seed), 3)
    return {
        "matrix_tiles": jnp.clip(jnp.exp(math.log(0.29882812) - 6.905664 * jax.random.uniform(arg_keys[0], (NB, S, B, B), jnp.float32) ** block_levels(arg_keys[0], (NB, S, B, B), ((0, 32),), -0.2, 0.2)), 0.00029945374, 0.29882812).astype(jnp.bfloat16),
        "pattern": draw_pattern(jax.random.fold_in(arg_keys[2], 71), 0),
    }


def merge_slots(products, flat_cols):
    slot_count = flat_cols.shape[0]
    matched_entries = flat_cols[:, None] == flat_cols[None, :]
    positions = jnp.arange(slot_count, dtype=jnp.int32)
    earlier = matched_entries & (positions[None, :] < positions[:, None])
    leading = jnp.logical_not(jnp.any(earlier, axis=1))
    weight = (matched_entries & leading[:, None]).astype(jnp.float32)
    return jnp.einsum("op,pac->oac", weight, products, precision=lax.Precision.HIGHEST)


def reference(matrix_tiles, pattern):
    tile_quantity = matrix_tiles.shape[0]
    slot_total = S * S
    column_index = jnp.take(pattern, pattern, axis=0).reshape(tile_quantity, slot_total)

    def expand_one(line_position):
        tile_row = matrix_tiles[line_position].astype(jnp.float32)
        targets = pattern[line_position]
        fetched = jnp.take(matrix_tiles, targets, axis=0).astype(jnp.float32)
        products = jnp.einsum("sab,stbc->stac", tile_row, fetched, precision=lax.Precision.HIGHEST)
        flattened = products.reshape(slot_total, B, B)
        merged = merge_slots(flattened, column_index[line_position])
        grown_similarity = merged.astype(jnp.bfloat16)
        squares = jnp.sum(jnp.square(grown_similarity.astype(jnp.float32)), axis=1)
        return grown_similarity, squares

    grown_similarity, squares = lax.map(expand_one, jnp.arange(tile_quantity, dtype=jnp.int32))
    totals = jax.ops.segment_sum(squares.reshape(tile_quantity * slot_total, B), column_index.reshape(-1), num_segments=tile_quantity)
    scale_factor = float(slot_total * B)

    def power_normalize_line(line_position):
        values = grown_similarity[line_position].astype(jnp.float32)
        needed = jnp.take(totals, column_index[line_position], axis=0)
        return (scale_factor * jnp.square(values) / needed[:, None, :]).astype(jnp.bfloat16)

    return lax.map(power_normalize_line, jnp.arange(tile_quantity, dtype=jnp.int32))
```

```python
import functools

import jax
import jax.numpy as jnp
from jax import lax
from jax.experimental import pallas as pl
from jax.experimental.pallas import tpu as pltpu
from jax.sharding import PartitionSpec as P

W = 2
AXES = ("row", "col", "depth")
CHUNKS = 4
FIELDS = 24


def both_ways(pairs):
    return pairs + [(b, a) for a, b in pairs]


def plan(pattern, start, rows_here, core):
    row_cols = lax.dynamic_slice_in_dim(pattern, start, rows_here, 0)
    slots = pattern.shape[1]
    out_cols = jnp.take(pattern, row_cols, axis=0).reshape(rows_here, slots * slots)
    offset = row_cols - start
    inside = (offset >= 0) & (offset < rows_here)
    above = offset >= rows_here
    beside = jnp.where(core == 0, above, offset < 0)
    source = jnp.where(inside, 0, jnp.where(beside, 1, 2))
    line = jnp.where(inside, offset, jnp.where(above, offset - rows_here, offset + rows_here))
    positions = jnp.arange(slots * slots, dtype=jnp.int32)
    matched = out_cols[:, :, None] == out_cols[:, None, :]
    lead = jnp.min(jnp.where(matched, positions[None, None, :], slots * slots), axis=2)
    window = out_cols - (start - core * rows_here - 2 * W)
    return jnp.concatenate([source, line, lead, window], axis=1).astype(jnp.int32).reshape(-1)


def expand_kernel(q, rows_here, slots, meta, own, beside, across, before, out, win, acc, right):
    del before
    width = across.shape[3]
    cols = slice(q * width, (q + 1) * width)
    win[...] = jnp.zeros_like(win)
    for r in range(rows_here):
        base = r * FIELDS
        for s in range(slots):
            if s == 0:
                for t in range(slots):
                    right[:, t * width : (t + 1) * width] = own[r, t, :, cols]
            else:
                source = meta[base + s]
                line = meta[base + slots + s]

                @pl.when(source == 0)
                def _():
                    for t in range(slots):
                        right[:, t * width : (t + 1) * width] = own[line, t, :, cols]

                @pl.when(source == 1)
                def _():
                    for t in range(slots):
                        right[:, t * width : (t + 1) * width] = beside[line, t, :, cols]

                @pl.when(source == 2)
                def _():
                    for t in range(slots):
                        right[:, t * width : (t + 1) * width] = across[line, t]

            product = jnp.dot(own[r, s], right[...], preferred_element_type=jnp.float32)
            for t in range(slots):
                part = product[:, t * width : (t + 1) * width]
                slot = s * slots + t
                if s == 0:
                    acc[slot] = part
                else:
                    lead = meta[base + 2 * slots + slot]

                    @pl.when(lead == slot)
                    def _():
                        acc[slot] = part

                    @pl.when(lead != slot)
                    def _():
                        acc[lead] += part
                        acc[slot] = jnp.zeros_like(part)

        for slot in range(slots * slots):
            values = acc[slot].astype(jnp.bfloat16)
            out[r, slot] = values
            wide = values.astype(jnp.float32)
            place = meta[base + 2 * slots + slots * slots + slot]
            win[pl.ds(place, 1), :] += jnp.sum(wide * wide, axis=0, keepdims=True)


def expand(q, meta, own, beside, across, before):
    rows_here, slots, side, width = across.shape
    vmem = pl.BlockSpec(memory_space=pltpu.VMEM)
    return pl.pallas_call(
        functools.partial(expand_kernel, q, rows_here, slots),
        in_specs=[pl.BlockSpec(memory_space=pltpu.SMEM), vmem, vmem, vmem, pl.BlockSpec(memory_space=pl.ANY)],
        out_specs=[vmem, vmem],
        out_shape=[
            jax.ShapeDtypeStruct((rows_here, slots * slots, side, width), jnp.bfloat16),
            jax.ShapeDtypeStruct((16, width), jnp.float32),
        ],
        scratch_shapes=[
            pltpu.VMEM((slots * slots, side, width), jnp.float32),
            pltpu.VMEM((side, slots * width), jnp.bfloat16),
        ],
        compiler_params=pltpu.CompilerParams(vmem_limit_bytes=24 * 2**20),
        cost_estimate=pl.CostEstimate(
            flops=2 * rows_here * slots * slots * side * side * width,
            bytes_accessed=12 * 2**20,
            transcendentals=0,
        ),
        name=f"expand{q}",
    )(meta, own, beside, across, before)


def inflate_kernel(scale, slots, group, meta, totals, *refs):
    parts, out = refs[:-1], refs[-1]
    width = parts[0].shape[3]
    r = pl.program_id(0)
    g = pl.program_id(1)
    for o in range(group):
        slot = g * group + o
        place = meta[r * FIELDS + 2 * slots + slots * slots + slot]
        factor = scale / totals[pl.ds(place, 1), :]
        for q, part in enumerate(parts):
            wide = part[r, slot].astype(jnp.float32)
            cols = slice(q * width, (q + 1) * width)
            out[0, o, :, cols] = (wide * wide * factor[:, cols]).astype(jnp.bfloat16)


def inflate(scale, slots, meta, totals, parts):
    rows_here, slot_total, side, width = parts[0].shape
    group = 3
    vmem = pl.BlockSpec(memory_space=pltpu.VMEM)
    return pl.pallas_call(
        functools.partial(inflate_kernel, scale, slots, group),
        grid=(rows_here, slot_total // group),
        in_specs=[pl.BlockSpec(memory_space=pltpu.SMEM), vmem] + [vmem] * len(parts),
        out_specs=pl.BlockSpec((1, group, side, width * len(parts)), lambda r, g: (r, g, 0, 0)),
        out_shape=jax.ShapeDtypeStruct((rows_here, slot_total, side, width * len(parts)), jnp.bfloat16),
        compiler_params=pltpu.CompilerParams(vmem_limit_bytes=24 * 2**20),
        cost_estimate=pl.CostEstimate(flops=2**24, bytes_accessed=18 * 2**20, transcendentals=0),
        name="inflate",
    )(meta, totals, *parts)


def shift_lines(block, distance):
    lines = block.shape[0]
    pad = jnp.zeros((abs(distance), block.shape[1]), block.dtype)
    if distance > 0:
        return jnp.concatenate([pad, block[: lines - distance]], axis=0)
    return jnp.concatenate([block[-distance:], pad], axis=0)


def body(matrix_tiles, pattern):
    rows_here, slots, side, _ = matrix_tiles.shape
    scale = float(slots * slots * side)
    devices = lax.axis_size(AXES)
    assert rows_here == W and lax.axis_size("depth") == 2
    core = lax.axis_index("depth")
    start = lax.axis_index(AXES) * rows_here
    chips = devices // 2
    swap = both_ways([(2 * c, 2 * c + 1) for c in range(chips)])
    next_chip = both_ways([(2 * c + 1, 2 * c + 2) for c in range(chips - 1)])
    second_chip = both_ways([(2 * c + 1, 2 * c + 4) for c in range(chips - 2)])

    width = side // CHUNKS
    across = [
        lax.ppermute(matrix_tiles[..., q * width : (q + 1) * width], AXES, next_chip)
        for q in range(CHUNKS)
    ]
    beside = lax.ppermute(matrix_tiles, AXES, swap)
    meta = plan(pattern, start, rows_here, core)
    parts, windows = [], []
    for q in range(CHUNKS):
        before = windows[-1] if windows else meta
        part, window = expand(q, meta, matrix_tiles, beside, across[q], before)
        parts.append(part)
        windows.append(window)
    window = jnp.concatenate(windows, axis=1)

    chip_rows = 2 * rows_here
    used = chip_rows + 4 * W
    window = window[:used]
    chip = window + lax.ppermute(window, AXES, swap)
    first = lax.ppermute(chip, AXES, next_chip)
    second = lax.ppermute(chip, AXES, second_chip)
    gathered = jnp.where(
        core == 0,
        shift_lines(first, -chip_rows) + shift_lines(second, -2 * chip_rows),
        shift_lines(first, chip_rows) + shift_lines(second, 2 * chip_rows),
    )
    totals = chip + gathered + lax.ppermute(gathered, AXES, swap)
    return inflate(scale, slots, meta, totals, parts)


def solution(mesh):
    return jax.shard_map(
        body,
        mesh=mesh,
        in_specs=(P(AXES, None, None, None), P()),
        out_specs=P(AXES, None, None, None),
        check_vma=False,
    )
```

```python
import functools

import jax
import jax.numpy as jnp
from jax import lax
from jax.experimental import pallas as pl
from jax.experimental.pallas import tpu as pltpu
from jax.sharding import PartitionSpec as P

W = 2
AXES = ("row", "col", "depth")
CHUNKS = 4
FIELDS = 24


def both_ways(pairs):
    return pairs + [(b, a) for a, b in pairs]


def plan(pattern, start, rows_here, core, kind):
    row_cols = lax.dynamic_slice_in_dim(pattern, start, rows_here, 0)
    slots = pattern.shape[1]
    out_cols = jnp.take(pattern, row_cols, axis=0).reshape(rows_here, slots * slots)
    offset = row_cols - start
    inside = (offset >= 0) & (offset < rows_here)
    above = offset >= rows_here
    beside = jnp.where(core == 0, above, offset < 0)
    source = jnp.where(inside, 0, jnp.where(beside, 1, 2))
    line = jnp.where(inside, offset, jnp.where(above, offset - rows_here, offset + rows_here))
    positions = jnp.arange(slots * slots, dtype=jnp.int32)
    matched = out_cols[:, :, None] == out_cols[:, None, :]
    lead = jnp.min(jnp.where(matched, positions[None, None, :], slots * slots), axis=2)
    window = out_cols - (start - core * rows_here - 2 * W)
    scalars = jnp.concatenate([source, line, lead, window], axis=1).astype(jnp.int32).reshape(-1)
    return jnp.concatenate([scalars, kind.astype(jnp.int32)[None]])


def detours(last_row, columns):
    def device(row, col, core):
        return (row * columns + col) * 2 + core

    top = columns - 1
    spare_up, spare_down = [device(0, 0, 0), device(0, 0, 1)], [device(last_row, top, 1), device(last_row, top, 0)]
    first, second, kinds = [], [], {}
    legs = [(first, []), (second, [])]
    for row in range(last_row):
        low, high = device(row, top, 1), device(row + 1, 0, 0)
        for source, target, spare, turn in ((high, low, spare_up, row), (low, high, spare_down, last_row - 1 - row)):
            which = turn // 2
            stop = spare[turn % 2]
            legs[which][0].append((source, stop))
            legs[which][1].append((stop, target))
            kinds[target] = which + 1
    return legs, kinds


def expand_kernel(q, rows_here, slots, meta, own, *refs):
    out, win, acc, right, sems = refs[-5:]
    beside, across = refs[0], refs[1:-6]
    width = out.shape[3]
    cols = pl.ds(q * width, width)

    def fetch(r, s):
        source, line = meta[r * FIELDS + s], meta[r * FIELDS + slots + s]
        if len(across) > 1:
            source = jnp.where(source == 2, 2 + meta[rows_here * FIELDS], source)
        job = r * (slots - 1) + s - 1
        places = [own.at[line, :, :, cols], beside.at[line, :, :, cols]] + [part.at[line] for part in across]
        for number, place in enumerate(places):

            @pl.when(source == number)
            def _():
                pltpu.make_async_copy(place, right.at[job], sems.at[job]).start()

    for r in range(rows_here):
        for s in range(1, slots):
            fetch(r, s)
    win[...] = jnp.zeros_like(win)

    def product(r, s, tiles):
        return jnp.dot(own[r, s], jnp.concatenate(tiles, axis=1), preferred_element_type=jnp.float32)

    def finish(r, slot, total):
        values = total.astype(jnp.bfloat16)
        out[r, slot] = values
        wide = values.astype(jnp.float32)
        place = meta[r * FIELDS + 2 * slots + slots * slots + slot]
        win[pl.ds(place, 1), :] += jnp.sum(wide * wide, axis=0, keepdims=True)

    for r in range(rows_here):
        first = product(r, 0, [own[r, t, :, cols] for t in range(slots)])
        for t in range(slots):
            acc[r, t] = first[:, t * width : (t + 1) * width]
    for r in range(rows_here):
        for s in range(1, slots):
            job = r * (slots - 1) + s - 1
            pltpu.make_async_copy(across[0].at[0], right.at[job], sems.at[job]).wait()
            later = product(r, s, [right[job, t] for t in range(slots)])
            for t in range(slots):
                part = later[:, t * width : (t + 1) * width]
                slot = s * slots + t
                lead = meta[r * FIELDS + 2 * slots + slot]

                @pl.when(lead == slot)
                def _():
                    if s == slots - 1:
                        finish(r, slot, part)
                    else:
                        acc[r, slot] = part

                @pl.when(lead != slot)
                def _():
                    acc[r, lead] += part
                    if s == slots - 1:
                        out[r, slot] = jnp.zeros_like(out[r, slot])
                    else:
                        acc[r, slot] = jnp.zeros_like(part)

        for slot in range(slots * (slots - 1)):
            finish(r, slot, acc[r, slot])


def expand(q, meta, own, beside, across, before):
    rows_here, slots, side, width = across[0].shape
    vmem, anywhere = pl.BlockSpec(memory_space=pltpu.VMEM), pl.BlockSpec(memory_space=pl.ANY)
    jobs = rows_here * (slots - 1)
    return pl.pallas_call(
        functools.partial(expand_kernel, q, rows_here, slots),
        in_specs=[pl.BlockSpec(memory_space=pltpu.SMEM), vmem] + [anywhere] * (len(across) + 2),
        out_specs=[vmem, vmem],
        out_shape=[
            jax.ShapeDtypeStruct((rows_here, slots * slots, side, width), jnp.bfloat16),
            jax.ShapeDtypeStruct((16, width), jnp.float32),
        ],
        scratch_shapes=[
            pltpu.VMEM((rows_here, slots * (slots - 1), side, width), jnp.float32),
            pltpu.VMEM((jobs, slots, side, width), jnp.bfloat16),
            pltpu.SemaphoreType.DMA((jobs,)),
        ],
        compiler_params=pltpu.CompilerParams(vmem_limit_bytes=24 * 2**20),
        cost_estimate=pl.CostEstimate(
            flops=2 * rows_here * slots * slots * side * side * width,
            bytes_accessed=12 * 2**20,
            transcendentals=0,
        ),
        name=f"expand{q}",
    )(meta, own, beside, *across, before)


def inflate_kernel(scale, slots, group, meta, totals, *refs):
    parts, out = refs[:-1], refs[-1]
    width = parts[0].shape[3]
    r = pl.program_id(0)
    g = pl.program_id(1)
    for o in range(group):
        slot = g * group + o
        place = meta[r * FIELDS + 2 * slots + slots * slots + slot]
        factor = scale / totals[pl.ds(place, 1), :]
        for q, part in enumerate(parts):
            wide = part[r, slot].astype(jnp.float32)
            cols = slice(q * width, (q + 1) * width)
            out[0, o, :, cols] = (wide * wide * factor[:, cols]).astype(jnp.bfloat16)


def inflate(scale, slots, meta, totals, parts):
    rows_here, slot_total, side, width = parts[0].shape
    group = 3
    vmem = pl.BlockSpec(memory_space=pltpu.VMEM)
    return pl.pallas_call(
        functools.partial(inflate_kernel, scale, slots, group),
        grid=(rows_here, slot_total // group),
        in_specs=[pl.BlockSpec(memory_space=pltpu.SMEM), vmem] + [vmem] * len(parts),
        out_specs=pl.BlockSpec((1, group, side, width * len(parts)), lambda r, g: (r, g, 0, 0)),
        out_shape=jax.ShapeDtypeStruct((rows_here, slot_total, side, width * len(parts)), jnp.bfloat16),
        compiler_params=pltpu.CompilerParams(vmem_limit_bytes=24 * 2**20),
        cost_estimate=pl.CostEstimate(flops=2**24, bytes_accessed=18 * 2**20, transcendentals=0),
        name="inflate",
    )(meta, totals, *parts)


def shift_lines(block, distance):
    lines = block.shape[0]
    pad = jnp.zeros((abs(distance), block.shape[1]), block.dtype)
    if distance > 0:
        return jnp.concatenate([pad, block[: lines - distance]], axis=0)
    return jnp.concatenate([block[-distance:], pad], axis=0)


def body(matrix_tiles, pattern):
    rows_here, slots, side, _ = matrix_tiles.shape
    scale = float(slots * slots * side)
    devices = lax.axis_size(AXES)
    assert rows_here == W and lax.axis_size("depth") == 2
    core = lax.axis_index("depth")
    start = lax.axis_index(AXES) * rows_here
    chips = devices // 2
    swap = both_ways([(2 * c, 2 * c + 1) for c in range(chips)])
    next_chip = both_ways([(2 * c + 1, 2 * c + 2) for c in range(chips - 1)])
    second_chip = both_ways([(2 * c + 1, 2 * c + 4) for c in range(chips - 2)])

    width = side // CHUNKS
    here = lax.axis_index(AXES)
    rows, columns = lax.axis_size("row"), lax.axis_size("col")
    pieces = [matrix_tiles[..., :width]]
    first, held = lax.optimization_barrier((pieces[0], matrix_tiles))
    pieces = [first] + [held[..., q * width : (q + 1) * width] for q in range(1, CHUNKS)]
    beside = lax.ppermute(matrix_tiles, AXES, swap)
    across = [[lax.ppermute(piece, AXES, next_chip)] for piece in pieces[:-1]]
    kind = jnp.int32(0)
    if rows == 4:
        legs, kinds = detours(rows - 1, columns)
        straight = [pair for pair in next_chip if pair[1] not in kinds]
        across.append([lax.ppermute(pieces[-1], AXES, straight)])
        for out_leg, home_leg in legs:
            across[-1].append(lax.ppermute(lax.ppermute(pieces[-1], AXES, out_leg), AXES, home_leg))
        for target, number in kinds.items():
            kind = jnp.where(here == target, number, kind)
    else:
        across.append([lax.ppermute(pieces[-1], AXES, next_chip)])
    meta = plan(pattern, start, rows_here, core, kind)
    parts, windows = [], []
    for q in range(CHUNKS):
        before = windows[-1] if windows else meta
        part, window = expand(q, meta, matrix_tiles, beside, across[q], before)
        parts.append(part)
        windows.append(window)
    window = jnp.concatenate(windows, axis=1)

    chip_rows = 2 * rows_here
    used = chip_rows + 4 * W
    window = window[:used]
    chip = window + lax.ppermute(window, AXES, swap)
    first = lax.ppermute(chip, AXES, next_chip)
    second = lax.ppermute(chip, AXES, second_chip)
    gathered = jnp.where(
        core == 0,
        shift_lines(first, -chip_rows) + shift_lines(second, -2 * chip_rows),
        shift_lines(first, chip_rows) + shift_lines(second, 2 * chip_rows),
    )
    totals = chip + gathered + lax.ppermute(gathered, AXES, swap)
    return inflate(scale, slots, meta, totals, parts)


def solution(mesh):
    return jax.shard_map(
        body,
        mesh=mesh,
        in_specs=(P(AXES, None, None, None), P()),
        out_specs=P(AXES, None, None, None),
        check_vma=False,
    )
```

```python
import functools

import jax
import jax.numpy as jnp
from jax import lax
from jax.experimental import pallas as pl
from jax.experimental.pallas import tpu as pltpu
from jax.sharding import PartitionSpec as P

W = 2
AXES = ("row", "col", "depth")
CHUNKS = 4
FIELDS = 24


def both_ways(pairs):
    return pairs + [(b, a) for a, b in pairs]


def plan(pattern, start, rows_here, core, kind):
    row_cols = lax.dynamic_slice_in_dim(pattern, start, rows_here, 0)
    slots = pattern.shape[1]
    out_cols = jnp.take(pattern, row_cols, axis=0).reshape(rows_here, slots * slots)
    offset = row_cols - start
    inside = (offset >= 0) & (offset < rows_here)
    above = offset >= rows_here
    beside = jnp.where(core == 0, above, offset < 0)
    source = jnp.where(inside, 0, jnp.where(beside, 1, 2))
    line = jnp.where(inside, offset, jnp.where(above, offset - rows_here, offset + rows_here))
    positions = jnp.arange(slots * slots, dtype=jnp.int32)
    matched = out_cols[:, :, None] == out_cols[:, None, :]
    lead = jnp.min(jnp.where(matched, positions[None, None, :], slots * slots), axis=2)
    window = out_cols - (start - core * rows_here - 2 * W)
    scalars = jnp.concatenate([source, line, lead, window], axis=1).astype(jnp.int32).reshape(-1)
    return jnp.concatenate([scalars, kind.astype(jnp.int32)[None]])


def detours(last_row, columns):
    def device(row, col, core):
        return (row * columns + col) * 2 + core

    top = columns - 1
    spare_up, spare_down = [device(0, 0, 0), device(0, 0, 1)], [device(last_row, top, 1), device(last_row, top, 0)]
    first, second, kinds = [], [], {}
    legs = [(first, []), (second, [])]
    for row in range(last_row):
        low, high = device(row, top, 1), device(row + 1, 0, 0)
        for source, target, spare, turn in ((high, low, spare_up, row), (low, high, spare_down, last_row - 1 - row)):
            which = min(turn, 1)
            stop = spare[max(turn - 1, 0)]
            legs[which][0].append((source, stop))
            legs[which][1].append((stop, target))
            kinds[target] = which + 1
    return legs, kinds


def expand_kernel(q, rows_here, slots, meta, own, *refs):
    out, win, acc, right, sems = refs[-5:]
    beside, across = refs[0], refs[1:-6]
    width = out.shape[3]
    cols = pl.ds(q * width, width)

    def fetch(r, s):
        source, line = meta[r * FIELDS + s], meta[r * FIELDS + slots + s]
        if len(across) > 1:
            source = jnp.where(source == 2, 2 + meta[rows_here * FIELDS], source)
        job = r * (slots - 1) + s - 1
        places = [own.at[line, :, :, cols], beside.at[line, :, :, cols]] + [part.at[line] for part in across]
        for number, place in enumerate(places):

            @pl.when(source == number)
            def _():
                pltpu.make_async_copy(place, right.at[job], sems.at[job]).start()

    for r in range(rows_here):
        for s in range(1, slots):
            fetch(r, s)
    win[...] = jnp.zeros_like(win)

    def product(r, s, tiles):
        return jnp.dot(own[r, s], jnp.concatenate(tiles, axis=1), preferred_element_type=jnp.float32)

    def finish(r, slot, total):
        values = total.astype(jnp.bfloat16)
        out[r, slot] = values
        wide = values.astype(jnp.float32)
        place = meta[r * FIELDS + 2 * slots + slots * slots + slot]
        win[pl.ds(place, 1), :] += jnp.sum(wide * wide, axis=0, keepdims=True)

    for r in range(rows_here):
        first = product(r, 0, [own[r, t, :, cols] for t in range(slots)])
        for t in range(slots):
            acc[r, t] = first[:, t * width : (t + 1) * width]
    for r in range(rows_here):
        for s in range(1, slots):
            job = r * (slots - 1) + s - 1
            pltpu.make_async_copy(across[0].at[0], right.at[job], sems.at[job]).wait()
            later = product(r, s, [right[job, t] for t in range(slots)])
            for t in range(slots):
                part = later[:, t * width : (t + 1) * width]
                slot = s * slots + t
                lead = meta[r * FIELDS + 2 * slots + slot]
                kept = part * jnp.where(lead == slot, 1.0, 0.0)
                acc[r, jnp.where(lead == slot, slots * (slots - 1), lead)] += part
                if s == slots - 1:
                    finish(r, slot, kept)
                else:
                    acc[r, slot] = kept

        for slot in range(slots * (slots - 1)):
            finish(r, slot, acc[r, slot])


def expand(q, meta, own, beside, across, before):
    rows_here, slots, side, width = across[0].shape
    vmem, anywhere = pl.BlockSpec(memory_space=pltpu.VMEM), pl.BlockSpec(memory_space=pl.ANY)
    jobs = rows_here * (slots - 1)
    return pl.pallas_call(
        functools.partial(expand_kernel, q, rows_here, slots),
        in_specs=[pl.BlockSpec(memory_space=pltpu.SMEM), vmem] + [anywhere] * (len(across) + 2),
        out_specs=[vmem, vmem],
        out_shape=[
            jax.ShapeDtypeStruct((rows_here, slots * slots, side, width), jnp.bfloat16),
            jax.ShapeDtypeStruct((16, width), jnp.float32),
        ],
        scratch_shapes=[
            pltpu.VMEM((rows_here, slots * (slots - 1) + 1, side, width), jnp.float32),
            pltpu.VMEM((jobs, slots, side, width), jnp.bfloat16),
            pltpu.SemaphoreType.DMA((jobs,)),
        ],
        compiler_params=pltpu.CompilerParams(vmem_limit_bytes=24 * 2**20),
        cost_estimate=pl.CostEstimate(
            flops=2 * rows_here * slots * slots * side * side * width,
            bytes_accessed=12 * 2**20,
            transcendentals=0,
        ),
        name=f"expand{q}",
    )(meta, own, beside, *across, before)


def inflate_kernel(scale, slots, first, meta, totals, *refs):
    count = len(refs) - 3 - (1 if first else 0)
    parts, (out, made, sems) = refs[:count], refs[-3:]
    rows_here, slot_total, side, width = parts[0].shape
    depth = made.shape[0]
    cols = pl.ds(first * width, count * width)
    jobs = [(r, slot) for r in range(rows_here) for slot in range(slot_total)]

    def sending(number):
        r, slot = jobs[number]
        at = number % depth
        return pltpu.make_async_copy(made.at[at], out.at[r, slot, :, cols], sems.at[at])

    for number, (r, slot) in enumerate(jobs):
        if number >= depth:
            sending(number - depth).wait()
        place = meta[r * FIELDS + 2 * slots + slots * slots + slot]
        factor = scale / totals[pl.ds(place, 1), :]
        for q, part in enumerate(parts):
            wide = part[r, slot].astype(jnp.float32)
            here = slice(q * width, (q + 1) * width)
            made[number % depth, :, here] = (wide * wide * factor[:, here]).astype(jnp.bfloat16)
        sending(number).start()
    for number in range(len(jobs) - depth, len(jobs)):
        sending(number).wait()


def inflate(scale, slots, meta, totals, parts, first=0, so_far=None):
    rows_here, slot_total, side, width = parts[0].shape
    vmem, anywhere = pl.BlockSpec(memory_space=pltpu.VMEM), pl.BlockSpec(memory_space=pl.ANY)
    more = [] if so_far is None else [so_far]
    return pl.pallas_call(
        functools.partial(inflate_kernel, scale, slots, first),
        in_specs=[pl.BlockSpec(memory_space=pltpu.SMEM), vmem] + [vmem] * len(parts) + [anywhere] * len(more),
        out_specs=anywhere,
        out_shape=jax.ShapeDtypeStruct((rows_here, slot_total, side, width * CHUNKS), jnp.bfloat16),
        scratch_shapes=[
            pltpu.VMEM((9, side, width * len(parts)), jnp.bfloat16),
            pltpu.SemaphoreType.DMA((9,)),
        ],
        input_output_aliases={2 + len(parts): 0} if more else {},
        compiler_params=pltpu.CompilerParams(vmem_limit_bytes=12 * 2**20),
        cost_estimate=pl.CostEstimate(flops=2**22 * len(parts), bytes_accessed=4 * 2**20 * len(parts), transcendentals=0),
        name=f"inflate{first}",
    )(meta, totals, *parts, *more)


def columns_kernel(q, width, tiles, *refs):
    out, sem = refs[-2:]
    copy = pltpu.make_async_copy(tiles.at[:, :, :, pl.ds(q * width, width)], out, sem)
    copy.start()
    copy.wait()


def columns_of(tiles, q, width, after):
    anywhere, far = pl.BlockSpec(memory_space=pl.ANY), pl.BlockSpec(memory_space=pltpu.HBM)
    return pl.pallas_call(
        functools.partial(columns_kernel, q, width),
        in_specs=[far] + [anywhere] * len(after),
        out_specs=far,
        out_shape=jax.ShapeDtypeStruct((*tiles.shape[:3], width), tiles.dtype),
        scratch_shapes=[pltpu.SemaphoreType.DMA],
        compiler_params=pltpu.CompilerParams(vmem_limit_bytes=2**20),
        cost_estimate=pl.CostEstimate(flops=0, bytes_accessed=2**20, transcendentals=0),
        name=f"columns{q}",
    )(tiles, *after)


def shift_lines(block, distance):
    lines = block.shape[0]
    pad = jnp.zeros((abs(distance), block.shape[1]), block.dtype)
    if distance > 0:
        return jnp.concatenate([pad, block[: lines - distance]], axis=0)
    return jnp.concatenate([block[-distance:], pad], axis=0)


def body(matrix_tiles, pattern):
    rows_here, slots, side, _ = matrix_tiles.shape
    scale = float(slots * slots * side)
    devices = lax.axis_size(AXES)
    assert rows_here == W and lax.axis_size("depth") == 2
    core = lax.axis_index("depth")
    start = lax.axis_index(AXES) * rows_here
    chips = devices // 2
    swap = both_ways([(2 * c, 2 * c + 1) for c in range(chips)])
    next_chip = both_ways([(2 * c + 1, 2 * c + 2) for c in range(chips - 1)])
    second_chip = both_ways([(2 * c + 1, 2 * c + 4) for c in range(chips - 2)])

    width = side // CHUNKS
    here = lax.axis_index(AXES)
    rows, columns = lax.axis_size("row"), lax.axis_size("col")
    beside = lax.ppermute(matrix_tiles, AXES, swap)
    pieces = [matrix_tiles[..., :width]] + [columns_of(matrix_tiles, q, width, [beside] * (q == 2)) for q in range(1, CHUNKS - 1)]
    kind = jnp.int32(0)
    if rows == 4:
        legs, kinds = detours(rows - 1, columns)
        straight = [pair for pair in next_chip if pair[1] not in kinds]
        side_leg = lax.ppermute(pieces[0], AXES, legs[1][0])
        stops = [lax.ppermute(pieces[0], AXES, straight + legs[0][0]), side_leg]
        first = [stops[0]] + [lax.ppermute(stop, AXES, home_leg) for stop, (_, home_leg) in zip(stops, legs)]
        for target, number in kinds.items():
            kind = jnp.where(here == target, number, kind)
        pieces.append(columns_of(matrix_tiles, CHUNKS - 1, width, stops))
        order = [*range(1, CHUNKS - 1), 0, CHUNKS - 1]
    else:
        first = [lax.ppermute(pieces[0], AXES, next_chip)]
        pieces.append(columns_of(matrix_tiles, CHUNKS - 1, width, first))
        order = [*range(CHUNKS)]
    across = [first] + [[lax.ppermute(piece, AXES, next_chip)] for piece in pieces[1:]]
    meta = plan(pattern, start, rows_here, core, kind)
    parts, windows = [None] * CHUNKS, [None] * CHUNKS
    before = meta
    for q in order:
        parts[q], windows[q] = expand(q, meta, matrix_tiles, beside, across[q], before)
        before = windows[q]
    window = jnp.concatenate(windows, axis=1)

    chip_rows = 2 * rows_here
    used = chip_rows + 4 * W
    window = window[:used]
    chip = window + lax.ppermute(window, AXES, swap)
    first = lax.ppermute(chip, AXES, next_chip)
    second = lax.ppermute(chip, AXES, second_chip)
    gathered = jnp.where(
        core == 0,
        shift_lines(first, -chip_rows) + shift_lines(second, -2 * chip_rows),
        shift_lines(first, chip_rows) + shift_lines(second, 2 * chip_rows),
    )
    totals = chip + gathered + lax.ppermute(gathered, AXES, swap)
    return inflate(scale, slots, meta, totals, parts)


def solution(mesh):
    return jax.shard_map(
        body,
        mesh=mesh,
        in_specs=(P(AXES, None, None, None), P()),
        out_specs=P(AXES, None, None, None),
        check_vma=False,
    )
```

```python
import functools

import jax
import jax.numpy as jnp
from jax import lax
from jax.experimental import pallas as pl
from jax.experimental.pallas import tpu as pltpu
from jax.sharding import PartitionSpec as P

W = 2
AXES = ("row", "col", "depth")
CHUNKS = 4
FIELDS = 24


def both_ways(pairs):
    return pairs + [(b, a) for a, b in pairs]


def plan(pattern, start, rows_here, core, kind):
    row_cols = lax.dynamic_slice_in_dim(pattern, start, rows_here, 0)
    slots = pattern.shape[1]
    out_cols = jnp.take(pattern, row_cols, axis=0).reshape(rows_here, slots * slots)
    offset = row_cols - start
    inside = (offset >= 0) & (offset < rows_here)
    above = offset >= rows_here
    beside = jnp.where(core == 0, above, offset < 0)
    source = jnp.where(inside, 0, jnp.where(beside, 1, 2))
    line = jnp.where(inside, offset, jnp.where(above, offset - rows_here, offset + rows_here))
    positions = jnp.arange(slots * slots, dtype=jnp.int32)
    matched = out_cols[:, :, None] == out_cols[:, None, :]
    lead = jnp.min(jnp.where(matched, positions[None, None, :], slots * slots), axis=2)
    window = out_cols - (start - core * rows_here - 2 * W)
    scalars = jnp.concatenate([source, line, lead, window], axis=1).astype(jnp.int32).reshape(-1)
    return jnp.concatenate([scalars, kind.astype(jnp.int32)[None]])


def detours(last_row, columns):
    def device(row, col, core):
        return (row * columns + col) * 2 + core

    top = columns - 1
    spare_up, spare_down = [device(0, 0, 0), device(0, 0, 1)], [device(last_row, top, 1), device(last_row, top, 0)]
    first, second, kinds = [], [], {}
    legs = [(first, []), (second, [])]
    for row in range(last_row):
        low, high = device(row, top, 1), device(row + 1, 0, 0)
        for source, target, spare, turn in ((high, low, spare_up, row), (low, high, spare_down, last_row - 1 - row)):
            which = 0 if turn == last_row - 1 else 1
            stop = spare[turn % 2]
            legs[which][0].append((source, stop))
            legs[which][1].append((stop, target))
            kinds[target] = which + 1
    return legs, kinds


def expand_kernel(q, rows_here, slots, meta, own, *refs):
    out, win, acc, right, sems = refs[-5:]
    beside, across = refs[0], refs[1:-6]
    width = out.shape[3]
    cols = pl.ds(q * width, width)

    def fetch(r, s):
        source, line = meta[r * FIELDS + s], meta[r * FIELDS + slots + s]
        if len(across) > 1:
            source = jnp.where(source == 2, 2 + meta[rows_here * FIELDS], source)
        job = r * (slots - 1) + s - 1
        places = [own.at[line, :, :, cols], beside.at[line, :, :, cols]] + [part.at[line] for part in across]
        for number, place in enumerate(places):

            @pl.when(source == number)
            def _():
                pltpu.make_async_copy(place, right.at[job], sems.at[job]).start()

    for r in range(rows_here):
        for s in range(1, slots):
            fetch(r, s)
    win[...] = jnp.zeros_like(win)

    def product(r, s, tiles):
        return jnp.dot(own[r, s], jnp.concatenate(tiles, axis=1), preferred_element_type=jnp.float32)

    def finish(r, slot, total):
        values = total.astype(jnp.bfloat16)
        out[r, slot] = values
        wide = values.astype(jnp.float32)
        place = meta[r * FIELDS + 2 * slots + slots * slots + slot]
        win[pl.ds(place, 1), :] += jnp.sum(wide * wide, axis=0, keepdims=True)

    for r in range(rows_here):
        first = product(r, 0, [own[r, t, :, cols] for t in range(slots)])
        for t in range(slots):
            acc[r, t] = first[:, t * width : (t + 1) * width]
    for r in range(rows_here):
        for s in range(1, slots):
            job = r * (slots - 1) + s - 1
            pltpu.make_async_copy(across[0].at[0], right.at[job], sems.at[job]).wait()
            later = product(r, s, [right[job, t] for t in range(slots)])
            for t in range(slots):
                part = later[:, t * width : (t + 1) * width]
                slot = s * slots + t
                lead = meta[r * FIELDS + 2 * slots + slot]
                kept = part * jnp.where(lead == slot, 1.0, 0.0)
                acc[r, jnp.where(lead == slot, slots * (slots - 1), lead)] += part
                if s == slots - 1:
                    finish(r, slot, kept)
                else:
                    acc[r, slot] = kept

        for slot in range(slots * (slots - 1)):
            finish(r, slot, acc[r, slot])


def expand(q, meta, own, beside, across, before):
    rows_here, slots, side, width = across[0].shape
    vmem, anywhere = pl.BlockSpec(memory_space=pltpu.VMEM), pl.BlockSpec(memory_space=pl.ANY)
    jobs = rows_here * (slots - 1)
    return pl.pallas_call(
        functools.partial(expand_kernel, q, rows_here, slots),
        in_specs=[pl.BlockSpec(memory_space=pltpu.SMEM), vmem] + [anywhere] * (len(across) + 2),
        out_specs=[vmem, vmem],
        out_shape=[
            jax.ShapeDtypeStruct((rows_here, slots * slots, side, width), jnp.bfloat16),
            jax.ShapeDtypeStruct((16, width), jnp.float32),
        ],
        scratch_shapes=[
            pltpu.VMEM((rows_here, slots * (slots - 1) + 1, side, width), jnp.float32),
            pltpu.VMEM((jobs, slots, side, width), jnp.bfloat16),
            pltpu.SemaphoreType.DMA((jobs,)),
        ],
        compiler_params=pltpu.CompilerParams(vmem_limit_bytes=24 * 2**20),
        cost_estimate=pl.CostEstimate(
            flops=2 * rows_here * slots * slots * side * side * width,
            bytes_accessed=12 * 2**20,
            transcendentals=0,
        ),
        name=f"expand{q}",
    )(meta, own, beside, *across, before)


def inflate_kernel(scale, slots, first, meta, totals, *refs):
    count = len(refs) - 3 - (1 if first else 0)
    parts, (out, made, sems) = refs[:count], refs[-3:]
    rows_here, slot_total, side, width = parts[0].shape
    depth = made.shape[0]
    cols = pl.ds(first * width, count * width)
    jobs = [(r, slot) for r in range(rows_here) for slot in range(slot_total)]

    def sending(number):
        r, slot = jobs[number]
        at = number % depth
        return pltpu.make_async_copy(made.at[at], out.at[r, slot, :, cols], sems.at[at])

    for number, (r, slot) in enumerate(jobs):
        if number >= depth:
            sending(number - depth).wait()
        place = meta[r * FIELDS + 2 * slots + slots * slots + slot]
        factor = scale / totals[pl.ds(place, 1), :]
        for q, part in enumerate(parts):
            wide = part[r, slot].astype(jnp.float32)
            here = slice(q * width, (q + 1) * width)
            made[number % depth, :, here] = (wide * wide * factor[:, here]).astype(jnp.bfloat16)
        sending(number).start()
    for number in range(len(jobs) - depth, len(jobs)):
        sending(number).wait()


def inflate(scale, slots, meta, totals, parts, first=0, so_far=None):
    rows_here, slot_total, side, width = parts[0].shape
    vmem, anywhere = pl.BlockSpec(memory_space=pltpu.VMEM), pl.BlockSpec(memory_space=pl.ANY)
    more = [] if so_far is None else [so_far]
    return pl.pallas_call(
        functools.partial(inflate_kernel, scale, slots, first),
        in_specs=[pl.BlockSpec(memory_space=pltpu.SMEM), vmem] + [vmem] * len(parts) + [anywhere] * len(more),
        out_specs=anywhere,
        out_shape=jax.ShapeDtypeStruct((rows_here, slot_total, side, width * CHUNKS), jnp.bfloat16),
        scratch_shapes=[
            pltpu.VMEM((9, side, width * len(parts)), jnp.bfloat16),
            pltpu.SemaphoreType.DMA((9,)),
        ],
        input_output_aliases={2 + len(parts): 0} if more else {},
        compiler_params=pltpu.CompilerParams(vmem_limit_bytes=12 * 2**20),
        cost_estimate=pl.CostEstimate(flops=2**22 * len(parts), bytes_accessed=4 * 2**20 * len(parts), transcendentals=0),
        name=f"inflate{first}",
    )(meta, totals, *parts, *more)


def columns_kernel(q, width, tiles, *refs):
    out, sem = refs[-2:]
    copy = pltpu.make_async_copy(tiles.at[:, :, :, pl.ds(q * width, width)], out, sem)
    copy.start()
    copy.wait()


def columns_of(tiles, q, width, after):
    anywhere, far = pl.BlockSpec(memory_space=pl.ANY), pl.BlockSpec(memory_space=pltpu.HBM)
    return pl.pallas_call(
        functools.partial(columns_kernel, q, width),
        in_specs=[far] + [anywhere] * len(after),
        out_specs=far,
        out_shape=jax.ShapeDtypeStruct((*tiles.shape[:3], width), tiles.dtype),
        scratch_shapes=[pltpu.SemaphoreType.DMA],
        compiler_params=pltpu.CompilerParams(vmem_limit_bytes=2**20),
        cost_estimate=pl.CostEstimate(flops=0, bytes_accessed=2**20, transcendentals=0),
        name=f"columns{q}",
    )(tiles, *after)


def shift_lines(block, distance):
    lines = block.shape[0]
    pad = jnp.zeros((abs(distance), block.shape[1]), block.dtype)
    if distance > 0:
        return jnp.concatenate([pad, block[: lines - distance]], axis=0)
    return jnp.concatenate([block[-distance:], pad], axis=0)


def body(matrix_tiles, pattern):
    rows_here, slots, side, _ = matrix_tiles.shape
    scale = float(slots * slots * side)
    devices = lax.axis_size(AXES)
    assert rows_here == W and lax.axis_size("depth") == 2
    core = lax.axis_index("depth")
    start = lax.axis_index(AXES) * rows_here
    chips = devices // 2
    swap = both_ways([(2 * c, 2 * c + 1) for c in range(chips)])
    next_chip = both_ways([(2 * c + 1, 2 * c + 2) for c in range(chips - 1)])
    second_chip = both_ways([(2 * c + 1, 2 * c + 4) for c in range(chips - 2)])

    width = side // CHUNKS
    here = lax.axis_index(AXES)
    rows, columns = lax.axis_size("row"), lax.axis_size("col")
    beside = lax.ppermute(matrix_tiles, AXES, swap)
    pieces = [matrix_tiles[..., :width]] + [columns_of(matrix_tiles, q, width, [beside] * (q == 2)) for q in range(1, CHUNKS - 1)]
    kind = jnp.int32(0)
    if rows == 4:
        legs, kinds = detours(rows - 1, columns)
        straight = [pair for pair in next_chip if pair[1] not in kinds]
        side_leg = lax.ppermute(columns_of(matrix_tiles, 0, width, [pieces[1]]), AXES, legs[1][0])
        stops = [lax.ppermute(pieces[0], AXES, straight + legs[0][0]), side_leg]
        first = [stops[0]] + [lax.ppermute(stop, AXES, home_leg) for stop, (_, home_leg) in zip(stops, legs)]
        for target, number in kinds.items():
            kind = jnp.where(here == target, number, kind)
        pieces.append(columns_of(matrix_tiles, CHUNKS - 1, width, stops))
        order = [*range(1, CHUNKS - 1), 0, CHUNKS - 1]
    else:
        first = [lax.ppermute(pieces[0], AXES, next_chip)]
        pieces.append(columns_of(matrix_tiles, CHUNKS - 1, width, first))
        order = [*range(CHUNKS)]
    across = [first] + [[lax.ppermute(piece, AXES, next_chip)] for piece in pieces[1:]]
    meta = plan(pattern, start, rows_here, core, kind)
    parts, windows = [None] * CHUNKS, [None] * CHUNKS
    before = meta
    for q in order:
        parts[q], windows[q] = expand(q, meta, matrix_tiles, beside, across[q], before)
        before = windows[q]
    window = jnp.concatenate(windows, axis=1)

    chip_rows = 2 * rows_here
    used = chip_rows + 4 * W
    window = window[:used]
    chip = window + lax.ppermute(window, AXES, swap)
    first = lax.ppermute(chip, AXES, next_chip)
    second = lax.ppermute(chip, AXES, second_chip)
    gathered = jnp.where(
        core == 0,
        shift_lines(first, -chip_rows) + shift_lines(second, -2 * chip_rows),
        shift_lines(first, chip_rows) + shift_lines(second, 2 * chip_rows),
    )
    totals = chip + gathered + lax.ppermute(gathered, AXES, swap)
    return inflate(scale, slots, meta, totals, parts)


def solution(mesh):
    return jax.shard_map(
        body,
        mesh=mesh,
        in_specs=(P(AXES, None, None, None), P()),
        out_specs=P(AXES, None, None, None),
        check_vma=False,
    )
```

```python
import functools

import jax
import jax.numpy as jnp
from jax import lax
from jax.experimental import pallas as pl
from jax.experimental.pallas import tpu as pltpu
from jax.sharding import PartitionSpec as P

W = 2
AXES = ("row", "col", "depth")
CHUNKS = 4
FIELDS = 33


def both_ways(pairs):
    return pairs + [(b, a) for a, b in pairs]


def plan(pattern, start, rows_here, core, kind):
    row_cols = lax.dynamic_slice_in_dim(pattern, start, rows_here, 0)
    slots = pattern.shape[1]
    out_cols = jnp.take(pattern, row_cols, axis=0).reshape(rows_here, slots * slots)
    offset = row_cols - start
    inside = (offset >= 0) & (offset < rows_here)
    above = offset >= rows_here
    beside = jnp.where(core == 0, above, offset < 0)
    source = jnp.where(inside, 0, jnp.where(beside, 1, 2))
    line = jnp.where(inside, offset, jnp.where(above, offset - rows_here, offset + rows_here))
    positions = jnp.arange(slots * slots, dtype=jnp.int32)
    matched = out_cols[:, :, None] == out_cols[:, None, :]
    lead = jnp.min(jnp.where(matched, positions[None, None, :], slots * slots), axis=2)
    window = out_cols - (start - core * rows_here - 2 * W)
    far = jnp.repeat(source == 2, slots, axis=1)
    touched = jnp.any(far[:, :, None] & (lead[:, :, None] == positions[None, None, :]), axis=1)
    scalars = jnp.concatenate([source, line, lead, window, touched], axis=1).astype(jnp.int32).reshape(-1)
    return jnp.concatenate([scalars, kind.astype(jnp.int32)[None]])


def detours(last_row, columns):
    def device(row, col, core):
        return (row * columns + col) * 2 + core

    top = columns - 1
    spare_up, spare_down = [device(0, 0, 0), device(0, 0, 1)], [device(last_row, top, 1), device(last_row, top, 0)]
    first, second, kinds = [], [], {}
    legs = [(first, []), (second, [])]
    for row in range(last_row):
        low, high = device(row, top, 1), device(row + 1, 0, 0)
        for source, target, spare, turn in ((high, low, spare_up, row), (low, high, spare_down, last_row - 1 - row)):
            which = 0 if turn == last_row - 1 else 1
            stop = spare[turn % 2]
            legs[which][0].append((source, stop))
            legs[which][1].append((stop, target))
            kinds[target] = which + 1
    return legs, kinds


def expand_kernel(q, rows_here, slots, meta, own, *refs):
    out, win, acc, right, sems = refs[-5:]
    beside, across = refs[0], refs[1:-6]
    width = out.shape[3]
    cols = pl.ds(q * width, width)

    def fetch(r, s):
        source, line = meta[r * FIELDS + s], meta[r * FIELDS + slots + s]
        if len(across) > 1:
            source = jnp.where(source == 2, 2 + meta[rows_here * FIELDS], source)
        job = r * (slots - 1) + s - 1
        places = [own.at[line, :, :, cols], beside.at[line, :, :, cols]] + [part.at[line] for part in across]
        for number, place in enumerate(places):

            @pl.when(source == number)
            def _():
                pltpu.make_async_copy(place, right.at[job], sems.at[job]).start()

    for r in range(rows_here):
        for s in range(1, slots):
            fetch(r, s)
    win[...] = jnp.zeros_like(win)

    def product(r, s, tiles):
        return jnp.dot(own[r, s], jnp.concatenate(tiles, axis=1), preferred_element_type=jnp.float32)

    def finish(r, slot, total):
        values = total.astype(jnp.bfloat16)
        out[r, slot] = values
        wide = values.astype(jnp.float32)
        place = meta[r * FIELDS + 2 * slots + slots * slots + slot]
        win[pl.ds(place, 1), :] += jnp.sum(wide * wide, axis=0, keepdims=True)

    for r in range(rows_here):
        first = product(r, 0, [own[r, t, :, cols] for t in range(slots)])
        for t in range(slots):
            acc[r, t] = first[:, t * width : (t + 1) * width]
    for r in range(rows_here):
        for s in range(1, slots):
            job = r * (slots - 1) + s - 1
            pltpu.make_async_copy(across[0].at[0], right.at[job], sems.at[job]).wait()
            later = product(r, s, [right[job, t] for t in range(slots)])
            for t in range(slots):
                part = later[:, t * width : (t + 1) * width]
                slot = s * slots + t
                lead = meta[r * FIELDS + 2 * slots + slot]
                kept = part * jnp.where(lead == slot, 1.0, 0.0)
                acc[r, jnp.where(lead == slot, slots * (slots - 1), lead)] += part
                if s == slots - 1:
                    finish(r, slot, kept)
                else:
                    acc[r, slot] = kept

        for slot in range(slots * (slots - 1)):
            finish(r, slot, acc[r, slot])


def split_kernel(q, rows_here, slots, late, meta, own, *refs):
    slot_total = slots * slots
    width = refs[0].shape[3] if late else refs[2].shape[3]
    cols = pl.ds(q * width, width)
    if late:
        acc_before, out_before, win_before = refs[:3]
        out, win, acc, right, sems = refs[-5:]
        across = refs[3:-6]
    else:
        beside = refs[0]
        acc, out, win, right, sems = refs[-5:]
    sources, lines = {}, {}
    jobs = [(r, s) for r in range(rows_here) for s in range(1, slots)]
    for job, (r, s) in enumerate(jobs):
        source, line = meta[r * FIELDS + s], meta[r * FIELDS + slots + s]
        if late:
            mine = source == 2
            which = meta[rows_here * FIELDS] if len(across) > 1 else 0
            places = [(mine & (which == number), part.at[line]) for number, part in enumerate(across)]
        else:
            mine = source != 2
            places = [(source == 0, own.at[line, :, :, cols]), (source == 1, beside.at[line, :, :, cols])]
        sources[job] = mine
        for chosen, place in places:

            @pl.when(chosen)
            def _():
                pltpu.make_async_copy(place, right.at[job], sems.at[job]).start()

    def field(r, group, slot):
        return meta[r * FIELDS + 2 * slots + group * slot_total + slot]

    def product(r, s, tiles):
        return jnp.dot(own[r, s], jnp.concatenate(tiles, axis=1), preferred_element_type=jnp.float32)

    def finish(r, slot):
        values = acc[r, slot].astype(jnp.bfloat16)
        out[r, slot] = values
        wide = values.astype(jnp.float32)
        win[pl.ds(field(r, 1, slot), 1), :] += jnp.sum(wide * wide, axis=0, keepdims=True)

    if late:
        win[...] = win_before[...]
        for r in range(rows_here):
            for slot in range(slot_total):
                touched = field(r, 2, slot) == 1

                @pl.when(touched)
                def _():
                    acc[r, slot] = acc_before[r, slot]

                @pl.when(jnp.logical_not(touched))
                def _():
                    out[r, slot] = out_before[r, slot]
    else:
        win[...] = jnp.zeros_like(win)
        for r in range(rows_here):
            first = product(r, 0, [own[r, t, :, cols] for t in range(slots)])
            for t in range(slots):
                acc[r, t] = first[:, t * width : (t + 1) * width]
            for slot in range(slots, slot_total):
                acc[r, slot] = jnp.zeros((acc.shape[2], width), jnp.float32)
    for job, (r, s) in enumerate(jobs):

        @pl.when(sources[job])
        def _():
            here = right.at[job]
            pltpu.make_async_copy(here, here, sems.at[job]).wait()
            later = product(r, s, [right[job, t] for t in range(slots)])
            for t in range(slots):
                acc[r, field(r, 0, s * slots + t)] += later[:, t * width : (t + 1) * width]

    for r in range(rows_here):
        for slot in range(slot_total):

            @pl.when(field(r, 2, slot) == (1 if late else 0))
            def _():
                finish(r, slot)


def expand_split(q, late, meta, own, inputs, before, width):
    rows_here, slots, side, _ = own.shape
    vmem, anywhere = pl.BlockSpec(memory_space=pltpu.VMEM), pl.BlockSpec(memory_space=pl.ANY)
    jobs = rows_here * (slots - 1)
    acc = jax.ShapeDtypeStruct((rows_here, slots * slots, side, width), jnp.float32)
    outs = [jax.ShapeDtypeStruct(acc.shape, jnp.bfloat16), jax.ShapeDtypeStruct((16, width), jnp.float32)]
    specs = [vmem] * 3 + [anywhere] * (len(inputs) - 3) if late else [anywhere] * len(inputs)
    return pl.pallas_call(
        functools.partial(split_kernel, q, rows_here, slots, late),
        in_specs=[pl.BlockSpec(memory_space=pltpu.SMEM), vmem] + specs + [anywhere],
        out_specs=[vmem] * (2 if late else 3),
        out_shape=outs if late else [acc] + outs,
        scratch_shapes=([pltpu.VMEM(acc.shape, jnp.float32)] if late else [])
        + [pltpu.VMEM((jobs, slots, side, width), jnp.bfloat16), pltpu.SemaphoreType.DMA((jobs,))],
        compiler_params=pltpu.CompilerParams(vmem_limit_bytes=12 * 2**20),
        cost_estimate=pl.CostEstimate(
            flops=rows_here * slots * slots * side * side * width,
            bytes_accessed=8 * 2**20,
            transcendentals=0,
        ),
        name=f"{'late' if late else 'early'}{q}",
    )(meta, own, *inputs, before)


def expand(q, meta, own, beside, across, before):
    rows_here, slots, side, width = across[0].shape
    vmem, anywhere = pl.BlockSpec(memory_space=pltpu.VMEM), pl.BlockSpec(memory_space=pl.ANY)
    jobs = rows_here * (slots - 1)
    return pl.pallas_call(
        functools.partial(expand_kernel, q, rows_here, slots),
        in_specs=[pl.BlockSpec(memory_space=pltpu.SMEM), vmem] + [anywhere] * (len(across) + 2),
        out_specs=[vmem, vmem],
        out_shape=[
            jax.ShapeDtypeStruct((rows_here, slots * slots, side, width), jnp.bfloat16),
            jax.ShapeDtypeStruct((16, width), jnp.float32),
        ],
        scratch_shapes=[
            pltpu.VMEM((rows_here, slots * (slots - 1) + 1, side, width), jnp.float32),
            pltpu.VMEM((jobs, slots, side, width), jnp.bfloat16),
            pltpu.SemaphoreType.DMA((jobs,)),
        ],
        compiler_params=pltpu.CompilerParams(vmem_limit_bytes=24 * 2**20),
        cost_estimate=pl.CostEstimate(
            flops=2 * rows_here * slots * slots * side * side * width,
            bytes_accessed=12 * 2**20,
            transcendentals=0,
        ),
        name=f"expand{q}",
    )(meta, own, beside, *across, before)


def inflate_kernel(scale, slots, first, meta, totals, *refs):
    count = len(refs) - 3 - (1 if first else 0)
    parts, (out, made, sems) = refs[:count], refs[-3:]
    rows_here, slot_total, side, width = parts[0].shape
    depth = made.shape[0]
    cols = pl.ds(first * width, count * width)
    jobs = [(r, slot) for r in range(rows_here) for slot in range(slot_total)]

    def sending(number):
        r, slot = jobs[number]
        at = number % depth
        return pltpu.make_async_copy(made.at[at], out.at[r, slot, :, cols], sems.at[at])

    for number, (r, slot) in enumerate(jobs):
        if number >= depth:
            sending(number - depth).wait()
        place = meta[r * FIELDS + 2 * slots + slots * slots + slot]
        factor = scale / totals[pl.ds(place, 1), :]
        for q, part in enumerate(parts):
            wide = part[r, slot].astype(jnp.float32)
            here = slice(q * width, (q + 1) * width)
            made[number % depth, :, here] = (wide * wide * factor[:, here]).astype(jnp.bfloat16)
        sending(number).start()
    for number in range(len(jobs) - depth, len(jobs)):
        sending(number).wait()


def inflate(scale, slots, meta, totals, parts, first=0, so_far=None):
    rows_here, slot_total, side, width = parts[0].shape
    vmem, anywhere = pl.BlockSpec(memory_space=pltpu.VMEM), pl.BlockSpec(memory_space=pl.ANY)
    more = [] if so_far is None else [so_far]
    return pl.pallas_call(
        functools.partial(inflate_kernel, scale, slots, first),
        in_specs=[pl.BlockSpec(memory_space=pltpu.SMEM), vmem] + [vmem] * len(parts) + [anywhere] * len(more),
        out_specs=anywhere,
        out_shape=jax.ShapeDtypeStruct((rows_here, slot_total, side, width * CHUNKS), jnp.bfloat16),
        scratch_shapes=[
            pltpu.VMEM((9, side, width * len(parts)), jnp.bfloat16),
            pltpu.SemaphoreType.DMA((9,)),
        ],
        input_output_aliases={2 + len(parts): 0} if more else {},
        compiler_params=pltpu.CompilerParams(vmem_limit_bytes=12 * 2**20),
        cost_estimate=pl.CostEstimate(flops=2**22 * len(parts), bytes_accessed=4 * 2**20 * len(parts), transcendentals=0),
        name=f"inflate{first}",
    )(meta, totals, *parts, *more)


def columns_kernel(q, width, tiles, *refs):
    out, sem = refs[-2:]
    copy = pltpu.make_async_copy(tiles.at[:, :, :, pl.ds(q * width, width)], out, sem)
    copy.start()
    copy.wait()


def columns_of(tiles, q, width, after):
    anywhere, far = pl.BlockSpec(memory_space=pl.ANY), pl.BlockSpec(memory_space=pltpu.HBM)
    return pl.pallas_call(
        functools.partial(columns_kernel, q, width),
        in_specs=[far] + [anywhere] * len(after),
        out_specs=far,
        out_shape=jax.ShapeDtypeStruct((*tiles.shape[:3], width), tiles.dtype),
        scratch_shapes=[pltpu.SemaphoreType.DMA],
        compiler_params=pltpu.CompilerParams(vmem_limit_bytes=2**20),
        cost_estimate=pl.CostEstimate(flops=0, bytes_accessed=2**20, transcendentals=0),
        name=f"columns{q}",
    )(tiles, *after)


def shift_lines(block, distance):
    lines = block.shape[0]
    pad = jnp.zeros((abs(distance), block.shape[1]), block.dtype)
    if distance > 0:
        return jnp.concatenate([pad, block[: lines - distance]], axis=0)
    return jnp.concatenate([block[-distance:], pad], axis=0)


def body(matrix_tiles, pattern):
    rows_here, slots, side, _ = matrix_tiles.shape
    scale = float(slots * slots * side)
    devices = lax.axis_size(AXES)
    assert rows_here == W and lax.axis_size("depth") == 2
    core = lax.axis_index("depth")
    start = lax.axis_index(AXES) * rows_here
    chips = devices // 2
    swap = both_ways([(2 * c, 2 * c + 1) for c in range(chips)])
    next_chip = both_ways([(2 * c + 1, 2 * c + 2) for c in range(chips - 1)])
    second_chip = both_ways([(2 * c + 1, 2 * c + 4) for c in range(chips - 2)])

    width = side // CHUNKS
    here = lax.axis_index(AXES)
    rows, columns = lax.axis_size("row"), lax.axis_size("col")
    beside = lax.ppermute(matrix_tiles, AXES, swap)
    pieces = [matrix_tiles[..., :width]]
    pieces.append(columns_of(matrix_tiles, 1, width, [pieces[0]]))
    pieces.append(columns_of(matrix_tiles, 2, width, [beside, pieces[1]]))
    kind = jnp.int32(0)
    if rows == 4:
        legs, kinds = detours(rows - 1, columns)
        straight = [pair for pair in next_chip if pair[1] not in kinds]
        side_leg = lax.ppermute(columns_of(matrix_tiles, 0, width, [pieces[1]]), AXES, legs[1][0])
        stops = [lax.ppermute(pieces[0], AXES, straight + legs[0][0]), side_leg]
        first = [stops[0]] + [lax.ppermute(stop, AXES, home_leg) for stop, (_, home_leg) in zip(stops, legs)]
        for target, number in kinds.items():
            kind = jnp.where(here == target, number, kind)
        follow = stops
        order = [*range(1, CHUNKS - 1), 0, CHUNKS - 1]
    else:
        first = [lax.ppermute(pieces[0], AXES, next_chip)]
        follow = first
        order = [*range(CHUNKS)]
    across = [first] + [[lax.ppermute(piece, AXES, next_chip)] for piece in pieces[1:]]
    meta = plan(pattern, start, rows_here, core, kind)
    parts, windows = [None] * CHUNKS, [None] * CHUNKS
    before = meta
    halves = {}
    for q in order[:-2]:
        parts[q], windows[q] = expand(q, meta, matrix_tiles, beside, across[q], before)
        before = windows[q]
        if q == order[0]:
            last = columns_of(matrix_tiles, CHUNKS - 1, width, [before, *follow])
            across.append([lax.ppermute(last, AXES, next_chip)])
        split = order[-1] if q == order[0] else order[-2]
        halves[split] = expand_split(split, False, meta, matrix_tiles, [beside], before, width)
        before = halves[split][2]
    for q in order[-2:]:
        parts[q], windows[q] = expand_split(q, True, meta, matrix_tiles, [*halves[q], *across[q]], before, width)
        before = windows[q]
    window = jnp.concatenate(windows, axis=1)

    chip_rows = 2 * rows_here
    used = chip_rows + 4 * W
    window = window[:used]
    chip = window + lax.ppermute(window, AXES, swap)
    first = lax.ppermute(chip, AXES, next_chip)
    second = lax.ppermute(chip, AXES, second_chip)
    gathered = jnp.where(
        core == 0,
        shift_lines(first, -chip_rows) + shift_lines(second, -2 * chip_rows),
        shift_lines(first, chip_rows) + shift_lines(second, 2 * chip_rows),
    )
    totals = chip + gathered + lax.ppermute(gathered, AXES, swap)
    return inflate(scale, slots, meta, totals, parts)


def solution(mesh):
    return jax.shard_map(
        body,
        mesh=mesh,
        in_specs=(P(AXES, None, None, None), P()),
        out_specs=P(AXES, None, None, None),
        check_vma=False,
    )
```

```python
import functools

import jax
import jax.numpy as jnp
from jax import lax
from jax.experimental import pallas as pl
from jax.experimental.pallas import tpu as pltpu
from jax.sharding import PartitionSpec as P

W = 2
AXES = ("row", "col", "depth")
CHUNKS = 4
FIELDS = 33


def both_ways(pairs):
    return pairs + [(b, a) for a, b in pairs]


def plan(pattern, start, rows_here, core, kind):
    row_cols = lax.dynamic_slice_in_dim(pattern, start, rows_here, 0)
    slots = pattern.shape[1]
    out_cols = jnp.take(pattern, row_cols, axis=0).reshape(rows_here, slots * slots)
    offset = row_cols - start
    inside = (offset >= 0) & (offset < rows_here)
    above = offset >= rows_here
    beside = jnp.where(core == 0, above, offset < 0)
    source = jnp.where(inside, 0, jnp.where(beside, 1, 2))
    line = jnp.where(inside, offset, jnp.where(above, offset - rows_here, offset + rows_here))
    positions = jnp.arange(slots * slots, dtype=jnp.int32)
    matched = out_cols[:, :, None] == out_cols[:, None, :]
    lead = jnp.min(jnp.where(matched, positions[None, None, :], slots * slots), axis=2)
    window = out_cols - (start - core * rows_here - 2 * W)
    far = jnp.repeat(source == 2, slots, axis=1)
    touched = jnp.any(far[:, :, None] & (lead[:, :, None] == positions[None, None, :]), axis=1)
    scalars = jnp.concatenate([source, line, lead, window, touched], axis=1).astype(jnp.int32).reshape(-1)
    return jnp.concatenate([scalars, kind.astype(jnp.int32)[None]])


def detours(last_row, columns):
    def device(row, col, core):
        return (row * columns + col) * 2 + core

    top = columns - 1
    spare_up, spare_down = [device(0, 0, 0), device(0, 0, 1)], [device(last_row, top, 1), device(last_row, top, 0)]
    first, second, kinds = [], [], {}
    legs = [(first, []), (second, [])]
    for row in range(last_row):
        low, high = device(row, top, 1), device(row + 1, 0, 0)
        for source, target, spare, turn in ((high, low, spare_up, row), (low, high, spare_down, last_row - 1 - row)):
            which = 0 if turn == last_row - 1 else 1
            stop = spare[turn % 2]
            legs[which][0].append((source, stop))
            legs[which][1].append((stop, target))
            kinds[target] = which + 1
    return legs, kinds


def expand_kernel(q, rows_here, slots, meta, own, *refs):
    out, win, acc, right, sems = refs[-5:]
    beside, across = refs[0], refs[1:-6]
    width = out.shape[3]
    cols = pl.ds(q * width, width)

    def fetch(r, s):
        source, line = meta[r * FIELDS + s], meta[r * FIELDS + slots + s]
        if len(across) > 1:
            source = jnp.where(source == 2, 2 + meta[rows_here * FIELDS], source)
        job = r * (slots - 1) + s - 1
        places = [own.at[line, :, :, cols], beside.at[line, :, :, cols]] + [part.at[line] for part in across]
        for number, place in enumerate(places):

            @pl.when(source == number)
            def _():
                pltpu.make_async_copy(place, right.at[job], sems.at[job]).start()

    for r in range(rows_here):
        for s in range(1, slots):
            fetch(r, s)
    win[...] = jnp.zeros_like(win)

    def product(r, s, tiles):
        return jnp.dot(own[r, s], jnp.concatenate(tiles, axis=1), preferred_element_type=jnp.float32)

    def finish(r, slot, total):
        values = total.astype(jnp.bfloat16)
        out[r, slot] = values
        wide = values.astype(jnp.float32)
        place = meta[r * FIELDS + 2 * slots + slots * slots + slot]
        win[pl.ds(place, 1), :] += jnp.sum(wide * wide, axis=0, keepdims=True)

    for r in range(rows_here):
        first = product(r, 0, [own[r, t, :, cols] for t in range(slots)])
        for t in range(slots):
            acc[r, t] = first[:, t * width : (t + 1) * width]
    for r in range(rows_here):
        for s in range(1, slots):
            job = r * (slots - 1) + s - 1
            pltpu.make_async_copy(across[0].at[0], right.at[job], sems.at[job]).wait()
            later = product(r, s, [right[job, t] for t in range(slots)])
            for t in range(slots):
                part = later[:, t * width : (t + 1) * width]
                slot = s * slots + t
                lead = meta[r * FIELDS + 2 * slots + slot]
                kept = part * jnp.where(lead == slot, 1.0, 0.0)
                acc[r, jnp.where(lead == slot, slots * (slots - 1), lead)] += part
                if s == slots - 1:
                    finish(r, slot, kept)
                else:
                    acc[r, slot] = kept

        for slot in range(slots * (slots - 1)):
            finish(r, slot, acc[r, slot])


def split_kernel(q, rows_here, slots, late, meta, own, *refs):
    slot_total = slots * slots
    width = refs[0].shape[3] if late else refs[2].shape[3]
    cols = pl.ds(q * width, width)
    if late:
        acc_before, out_before, win_before = refs[:3]
        out, win, acc, right, sems = refs[-5:]
        across = refs[3:-6]
    else:
        beside = refs[0]
        acc, out, win, right, sems = refs[-5:]
    sources, lines = {}, {}
    jobs = [(r, s) for r in range(rows_here) for s in range(1, slots)]
    for job, (r, s) in enumerate(jobs):
        source, line = meta[r * FIELDS + s], meta[r * FIELDS + slots + s]
        if late:
            mine = source == 2
            which = meta[rows_here * FIELDS] if len(across) > 1 else 0
            places = [(mine & (which == number), part.at[line]) for number, part in enumerate(across)]
        else:
            mine = source != 2
            places = [(source == 0, own.at[line, :, :, cols]), (source == 1, beside.at[line, :, :, cols])]
        sources[job] = mine
        for chosen, place in places:

            @pl.when(chosen)
            def _():
                pltpu.make_async_copy(place, right.at[job], sems.at[job]).start()

    def field(r, group, slot):
        return meta[r * FIELDS + 2 * slots + group * slot_total + slot]

    def product(r, s, tiles):
        return jnp.dot(own[r, s], jnp.concatenate(tiles, axis=1), preferred_element_type=jnp.float32)

    def finish(r, slot):
        values = acc[r, slot].astype(jnp.bfloat16)
        out[r, slot] = values
        wide = values.astype(jnp.float32)
        win[pl.ds(field(r, 1, slot), 1), :] += jnp.sum(wide * wide, axis=0, keepdims=True)

    if late:
        win[...] = win_before[...]
        for r in range(rows_here):
            for slot in range(slot_total):
                touched = field(r, 2, slot) == 1

                @pl.when(touched)
                def _():
                    acc[r, slot] = acc_before[r, slot]

                @pl.when(jnp.logical_not(touched))
                def _():
                    out[r, slot] = out_before[r, slot]
    else:
        win[...] = jnp.zeros_like(win)
        for r in range(rows_here):
            first = product(r, 0, [own[r, t, :, cols] for t in range(slots)])
            for t in range(slots):
                acc[r, t] = first[:, t * width : (t + 1) * width]
            for slot in range(slots, slot_total):
                acc[r, slot] = jnp.zeros((acc.shape[2], width), jnp.float32)
    for job, (r, s) in enumerate(jobs):

        @pl.when(sources[job])
        def _():
            here = right.at[job]
            pltpu.make_async_copy(here, here, sems.at[job]).wait()
            later = product(r, s, [right[job, t] for t in range(slots)])
            for t in range(slots):
                acc[r, field(r, 0, s * slots + t)] += later[:, t * width : (t + 1) * width]

    for r in range(rows_here):
        for slot in range(slot_total):

            @pl.when(field(r, 2, slot) == (1 if late else 0))
            def _():
                finish(r, slot)


def expand_split(q, late, meta, own, inputs, before, width):
    rows_here, slots, side, _ = own.shape
    vmem, anywhere = pl.BlockSpec(memory_space=pltpu.VMEM), pl.BlockSpec(memory_space=pl.ANY)
    jobs = rows_here * (slots - 1)
    acc = jax.ShapeDtypeStruct((rows_here, slots * slots, side, width), jnp.float32)
    outs = [jax.ShapeDtypeStruct(acc.shape, jnp.bfloat16), jax.ShapeDtypeStruct((16, width), jnp.float32)]
    specs = [vmem] * 3 + [anywhere] * (len(inputs) - 3) if late else [anywhere] * len(inputs)
    return pl.pallas_call(
        functools.partial(split_kernel, q, rows_here, slots, late),
        in_specs=[pl.BlockSpec(memory_space=pltpu.SMEM), vmem] + specs + [anywhere],
        out_specs=[vmem] * (2 if late else 3),
        out_shape=outs if late else [acc] + outs,
        scratch_shapes=([pltpu.VMEM(acc.shape, jnp.float32)] if late else [])
        + [pltpu.VMEM((jobs, slots, side, width), jnp.bfloat16), pltpu.SemaphoreType.DMA((jobs,))],
        compiler_params=pltpu.CompilerParams(vmem_limit_bytes=12 * 2**20),
        cost_estimate=pl.CostEstimate(
            flops=rows_here * slots * slots * side * side * width,
            bytes_accessed=8 * 2**20,
            transcendentals=0,
        ),
        name=f"{'late' if late else 'early'}{q}",
    )(meta, own, *inputs, before)


def expand(q, meta, own, beside, across, before):
    rows_here, slots, side, width = across[0].shape
    vmem, anywhere = pl.BlockSpec(memory_space=pltpu.VMEM), pl.BlockSpec(memory_space=pl.ANY)
    jobs = rows_here * (slots - 1)
    return pl.pallas_call(
        functools.partial(expand_kernel, q, rows_here, slots),
        in_specs=[pl.BlockSpec(memory_space=pltpu.SMEM), vmem] + [anywhere] * (len(across) + 2),
        out_specs=[vmem, vmem],
        out_shape=[
            jax.ShapeDtypeStruct((rows_here, slots * slots, side, width), jnp.bfloat16),
            jax.ShapeDtypeStruct((16, width), jnp.float32),
        ],
        scratch_shapes=[
            pltpu.VMEM((rows_here, slots * (slots - 1) + 1, side, width), jnp.float32),
            pltpu.VMEM((jobs, slots, side, width), jnp.bfloat16),
            pltpu.SemaphoreType.DMA((jobs,)),
        ],
        compiler_params=pltpu.CompilerParams(vmem_limit_bytes=24 * 2**20),
        cost_estimate=pl.CostEstimate(
            flops=2 * rows_here * slots * slots * side * side * width,
            bytes_accessed=12 * 2**20,
            transcendentals=0,
        ),
        name=f"expand{q}",
    )(meta, own, beside, *across, before)


def inflate_kernel(scale, slots, first, more, meta, totals, *refs):
    count = len(refs) - 3 - more
    parts, (out, made, sems) = refs[:count], refs[-3:]
    rows_here, slot_total, side, width = parts[0].shape
    depth = made.shape[0]
    cols = pl.ds(first * width, count * width)
    jobs = [(r, slot) for r in range(rows_here) for slot in range(slot_total)]

    def sending(number):
        r, slot = jobs[number]
        at = number % depth
        return pltpu.make_async_copy(made.at[at], out.at[r, slot, :, cols], sems.at[at])

    def leads(number):
        r, slot = jobs[number]
        return meta[r * FIELDS + 2 * slots + slot] == slot

    for number, (r, slot) in enumerate(jobs):
        if number >= depth:

            @pl.when(leads(number - depth))
            def _():
                sending(number - depth).wait()

        @pl.when(leads(number))
        def _():
            place = meta[r * FIELDS + 2 * slots + slots * slots + slot]
            factor = scale / totals[pl.ds(place, 1), :]
            for q, part in enumerate(parts):
                wide = part[r, slot].astype(jnp.float32)
                here = slice(q * width, (q + 1) * width)
                made[number % depth, :, here] = (wide * wide * factor[:, here]).astype(jnp.bfloat16)
            sending(number).start()

    for number in range(len(jobs) - depth, len(jobs)):

        @pl.when(leads(number))
        def _():
            sending(number).wait()


def inflate(scale, slots, meta, totals, parts, first=0, so_far=None):
    rows_here, slot_total, side, width = parts[0].shape
    vmem, anywhere = pl.BlockSpec(memory_space=pltpu.VMEM), pl.BlockSpec(memory_space=pl.ANY)
    more = [] if so_far is None else [so_far]
    return pl.pallas_call(
        functools.partial(inflate_kernel, scale, slots, first, len(more)),
        in_specs=[pl.BlockSpec(memory_space=pltpu.SMEM), vmem] + [vmem] * len(parts) + [anywhere] * len(more),
        out_specs=anywhere,
        out_shape=jax.ShapeDtypeStruct((rows_here, slot_total, side, width * CHUNKS), jnp.bfloat16),
        scratch_shapes=[
            pltpu.VMEM((9, side, width * len(parts)), jnp.bfloat16),
            pltpu.SemaphoreType.DMA((9,)),
        ],
        input_output_aliases={2 + len(parts): 0} if more else {},
        compiler_params=pltpu.CompilerParams(vmem_limit_bytes=12 * 2**20),
        cost_estimate=pl.CostEstimate(flops=2**22 * len(parts), bytes_accessed=4 * 2**20 * len(parts), transcendentals=0),
        name=f"inflate{first}",
    )(meta, totals, *parts, *more)


def blank_kernel(slots, meta, before, out, zero, sem):
    del before
    zero[...] = jnp.zeros_like(zero)
    jobs = [(r, slot) for r in range(out.shape[0]) for slot in range(out.shape[1])]
    for finish in (False, True):
        for number, (r, slot) in enumerate(jobs):

            @pl.when(meta[r * FIELDS + 2 * slots + slot] != slot)
            def _():
                copy = pltpu.make_async_copy(zero, out.at[r, slot], sem.at[number])
                copy.wait() if finish else copy.start()


def blank_slots(meta, before, rows_here, slots, side):
    anywhere = pl.BlockSpec(memory_space=pl.ANY)
    shape = (rows_here, slots * slots, side, side)
    return pl.pallas_call(
        functools.partial(blank_kernel, slots),
        in_specs=[pl.BlockSpec(memory_space=pltpu.SMEM), anywhere],
        out_specs=anywhere,
        out_shape=jax.ShapeDtypeStruct(shape, jnp.bfloat16),
        scratch_shapes=[pltpu.VMEM(shape[2:], jnp.bfloat16), pltpu.SemaphoreType.DMA((shape[0] * shape[1],))],
        compiler_params=pltpu.CompilerParams(vmem_limit_bytes=2 * 2**20),
        cost_estimate=pl.CostEstimate(flops=0, bytes_accessed=2**21, transcendentals=0),
        name="blank",
    )(meta, before)


def columns_kernel(q, width, tiles, *refs):
    out, sem = refs[-2:]
    copy = pltpu.make_async_copy(tiles.at[:, :, :, pl.ds(q * width, width)], out, sem)
    copy.start()
    copy.wait()


def columns_of(tiles, q, width, after):
    anywhere, far = pl.BlockSpec(memory_space=pl.ANY), pl.BlockSpec(memory_space=pltpu.HBM)
    return pl.pallas_call(
        functools.partial(columns_kernel, q, width),
        in_specs=[far] + [anywhere] * len(after),
        out_specs=far,
        out_shape=jax.ShapeDtypeStruct((*tiles.shape[:3], width), tiles.dtype),
        scratch_shapes=[pltpu.SemaphoreType.DMA],
        compiler_params=pltpu.CompilerParams(vmem_limit_bytes=2**20),
        cost_estimate=pl.CostEstimate(flops=0, bytes_accessed=2**20, transcendentals=0),
        name=f"columns{q}",
    )(tiles, *after)


def body(matrix_tiles, pattern):
    rows_here, slots, side, _ = matrix_tiles.shape
    scale = float(slots * slots * side)
    devices = lax.axis_size(AXES)
    assert rows_here == W and lax.axis_size("depth") == 2
    core = lax.axis_index("depth")
    start = lax.axis_index(AXES) * rows_here
    chips = devices // 2
    swap = both_ways([(2 * c, 2 * c + 1) for c in range(chips)])
    next_chip = both_ways([(2 * c + 1, 2 * c + 2) for c in range(chips - 1)])
    second_chip = both_ways([(2 * c + 1, 2 * c + 4) for c in range(chips - 2)])

    width = side // CHUNKS
    here = lax.axis_index(AXES)
    rows, columns = lax.axis_size("row"), lax.axis_size("col")
    beside = lax.ppermute(matrix_tiles, AXES, swap)
    pieces = [matrix_tiles[..., :width]]
    pieces.append(columns_of(matrix_tiles, 1, width, [pieces[0]]))
    pieces.append(columns_of(matrix_tiles, 2, width, [beside, pieces[1]]))
    kind = jnp.int32(0)
    if rows == 4:
        legs, kinds = detours(rows - 1, columns)
        straight = [pair for pair in next_chip if pair[1] not in kinds]
        side_leg = lax.ppermute(columns_of(matrix_tiles, 0, width, [pieces[1]]), AXES, legs[1][0])
        stops = [lax.ppermute(pieces[0], AXES, straight + legs[0][0]), side_leg]
        first = [stops[0]] + [lax.ppermute(stop, AXES, home_leg) for stop, (_, home_leg) in zip(stops, legs)]
        for target, number in kinds.items():
            kind = jnp.where(here == target, number, kind)
        follow = stops
        order = [*range(1, CHUNKS - 1), 0, CHUNKS - 1]
    else:
        first = [lax.ppermute(pieces[0], AXES, next_chip)]
        follow = first
        order = [*range(CHUNKS)]
    across = [first] + [[lax.ppermute(piece, AXES, next_chip)] for piece in pieces[1:]]
    meta = plan(pattern, start, rows_here, core, kind)
    parts, windows = [None] * CHUNKS, [None] * CHUNKS
    before = meta
    halves = {}
    for q in order[:-2]:
        parts[q], windows[q] = expand(q, meta, matrix_tiles, beside, across[q], before)
        before = windows[q]
        if q == order[0]:
            last = columns_of(matrix_tiles, CHUNKS - 1, width, [before, *follow])
            across.append([lax.ppermute(last, AXES, next_chip)])
        if q == order[0]:
            before = so_far = blank_slots(meta, last, rows_here, slots, side)
        split = order[-1] if q == order[0] else order[-2]
        halves[split] = expand_split(split, False, meta, matrix_tiles, [beside], before, width)
        before = halves[split][2]
    for q in order[-2:]:
        parts[q], windows[q] = expand_split(q, True, meta, matrix_tiles, [*halves[q], *across[q]], before, width)
        before = windows[q]
    window = jnp.concatenate(windows, axis=1)

    chip_rows = 2 * rows_here
    used = chip_rows + 4 * W
    window = window[:used]
    chip = window + lax.ppermute(window, AXES, swap)
    low = core == 0
    near, far = 2 * chip_rows, chip_rows
    first = lax.ppermute(jnp.where(low, chip[:near], chip[used - near :]), AXES, next_chip)
    second = lax.ppermute(jnp.where(low, chip[:far], chip[used - far :]), AXES, second_chip)
    blank = jnp.zeros((chip_rows, chip.shape[1]), chip.dtype)
    gathered = first + jnp.where(low, jnp.concatenate([second, blank]), jnp.concatenate([blank, second]))
    other = lax.ppermute(gathered, AXES, swap)
    below, above = jnp.where(low, gathered, other), jnp.where(low, other, gathered)
    totals = chip + jnp.concatenate([below, blank]) + jnp.concatenate([blank, above])
    return inflate(scale, slots, meta, totals, parts, so_far=so_far)


def solution(mesh):
    return jax.shard_map(
        body,
        mesh=mesh,
        in_specs=(P(AXES, None, None, None), P()),
        out_specs=P(AXES, None, None, None),
        check_vma=False,
    )
```

```python
import functools

import jax
import jax.numpy as jnp
from jax import lax
from jax.experimental import pallas as pl
from jax.experimental.pallas import tpu as pltpu
from jax.sharding import PartitionSpec as P

W = 2
AXES = ("row", "col", "depth")
CHUNKS = 4
FIELDS = 33


def both_ways(pairs):
    return pairs + [(b, a) for a, b in pairs]


def plan(pattern, start, rows_here, core, kind):
    row_cols = lax.dynamic_slice_in_dim(pattern, start, rows_here, 0)
    slots = pattern.shape[1]
    out_cols = jnp.take(pattern, row_cols, axis=0).reshape(rows_here, slots * slots)
    offset = row_cols - start
    inside = (offset >= 0) & (offset < rows_here)
    above = offset >= rows_here
    beside = jnp.where(core == 0, above, offset < 0)
    source = jnp.where(inside, 0, jnp.where(beside, 1, 2))
    line = jnp.where(inside, offset, jnp.where(above, offset - rows_here, offset + rows_here))
    positions = jnp.arange(slots * slots, dtype=jnp.int32)
    matched = out_cols[:, :, None] == out_cols[:, None, :]
    lead = jnp.min(jnp.where(matched, positions[None, None, :], slots * slots), axis=2)
    window = out_cols - (start - core * rows_here - 2 * W)
    far = jnp.repeat(source == 2, slots, axis=1)
    touched = jnp.any(far[:, :, None] & (lead[:, :, None] == positions[None, None, :]), axis=1)
    scalars = jnp.concatenate([source, line, lead, window, touched], axis=1).astype(jnp.int32).reshape(-1)
    return jnp.concatenate([scalars, kind.astype(jnp.int32)[None]])


def detours(last_row, columns):
    def device(row, col, core):
        return (row * columns + col) * 2 + core

    top = columns - 1
    spare_up, spare_down = [device(0, 0, 0), device(0, 0, 1)], [device(last_row, top, 1), device(last_row, top, 0)]
    first, second, kinds = [], [], {}
    legs = [(first, []), (second, [])]
    for row in range(last_row):
        low, high = device(row, top, 1), device(row + 1, 0, 0)
        for source, target, spare, turn in ((high, low, spare_up, row), (low, high, spare_down, last_row - 1 - row)):
            which = 0 if turn == last_row - 1 else 1
            stop = spare[turn % 2]
            legs[which][0].append((source, stop))
            legs[which][1].append((stop, target))
            kinds[target] = which + 1
    return legs, kinds


def expand_kernel(q, rows_here, slots, meta, own, *refs):
    out, win, acc, right, sems = refs[-5:]
    beside, across = refs[0], refs[1:-6]
    width = out.shape[3]
    cols = pl.ds(q * width, width)

    def fetch(r, s):
        source, line = meta[r * FIELDS + s], meta[r * FIELDS + slots + s]
        if len(across) > 1:
            source = jnp.where(source == 2, 2 + meta[rows_here * FIELDS], source)
        job = r * (slots - 1) + s - 1
        places = [own.at[line, :, :, cols], beside.at[line, :, :, cols]] + [part.at[line] for part in across]
        for number, place in enumerate(places):

            @pl.when(source == number)
            def _():
                pltpu.make_async_copy(place, right.at[job], sems.at[job]).start()

    for r in range(rows_here):
        for s in range(1, slots):
            fetch(r, s)
    win[...] = jnp.zeros_like(win)

    def product(r, s, tiles):
        return jnp.dot(own[r, s], jnp.concatenate(tiles, axis=1), preferred_element_type=jnp.float32)

    def finish(r, slot, total):
        values = total.astype(jnp.bfloat16)
        out[r, slot] = values
        wide = values.astype(jnp.float32)
        place = meta[r * FIELDS + 2 * slots + slots * slots + slot]
        win[pl.ds(place, 1), :] += jnp.sum(wide * wide, axis=0, keepdims=True)

    for r in range(rows_here):
        first = product(r, 0, [own[r, t, :, cols] for t in range(slots)])
        for t in range(slots):
            acc[r, t] = first[:, t * width : (t + 1) * width]
    for r in range(rows_here):
        for s in range(1, slots):
            job = r * (slots - 1) + s - 1
            pltpu.make_async_copy(across[0].at[0], right.at[job], sems.at[job]).wait()
            later = product(r, s, [right[job, t] for t in range(slots)])
            for t in range(slots):
                part = later[:, t * width : (t + 1) * width]
                slot = s * slots + t
                lead = meta[r * FIELDS + 2 * slots + slot]
                kept = part * jnp.where(lead == slot, 1.0, 0.0)
                acc[r, jnp.where(lead == slot, slots * (slots - 1), lead)] += part
                if s == slots - 1:
                    finish(r, slot, kept)
                else:
                    acc[r, slot] = kept

        for slot in range(slots * (slots - 1)):
            finish(r, slot, acc[r, slot])


def split_kernel(q, rows_here, slots, late, meta, own, *refs):
    slot_total = slots * slots
    width = refs[0].shape[3] if late else refs[2].shape[3]
    cols = pl.ds(q * width, width)
    if late:
        acc_before, out_before, win_before = refs[:3]
        out, win, acc, right, sems = refs[-5:]
        across = refs[3:-6]
    else:
        beside = refs[0]
        acc, out, win, right, sems = refs[-5:]
    sources, lines = {}, {}
    jobs = [(r, s) for r in range(rows_here) for s in range(1, slots)]
    for job, (r, s) in enumerate(jobs):
        source, line = meta[r * FIELDS + s], meta[r * FIELDS + slots + s]
        if late:
            mine = source == 2
            which = meta[rows_here * FIELDS] if len(across) > 1 else 0
            places = [(mine & (which == number), part.at[line]) for number, part in enumerate(across)]
        else:
            mine = source != 2
            places = [(source == 0, own.at[line, :, :, cols]), (source == 1, beside.at[line, :, :, cols])]
        sources[job] = mine
        for chosen, place in places:

            @pl.when(chosen)
            def _():
                pltpu.make_async_copy(place, right.at[job], sems.at[job]).start()

    def field(r, group, slot):
        return meta[r * FIELDS + 2 * slots + group * slot_total + slot]

    def product(r, s, tiles):
        return jnp.dot(own[r, s], jnp.concatenate(tiles, axis=1), preferred_element_type=jnp.float32)

    def finish(r, slot):
        values = acc[r, slot].astype(jnp.bfloat16)
        out[r, slot] = values
        wide = values.astype(jnp.float32)
        win[pl.ds(field(r, 1, slot), 1), :] += jnp.sum(wide * wide, axis=0, keepdims=True)

    if late:
        win[...] = win_before[...]
        for r in range(rows_here):
            for slot in range(slot_total):
                touched = field(r, 2, slot) == 1

                @pl.when(touched)
                def _():
                    acc[r, slot] = acc_before[r, slot]

                @pl.when(jnp.logical_not(touched) & (field(r, 0, slot) == slot))
                def _():
                    out[r, slot] = out_before[r, slot]
    else:
        win[...] = jnp.zeros_like(win)
        for r in range(rows_here):
            first = product(r, 0, [own[r, t, :, cols] for t in range(slots)])
            for t in range(slots):
                acc[r, t] = first[:, t * width : (t + 1) * width]
            for slot in range(slots, slot_total):
                acc[r, slot] = jnp.zeros((acc.shape[2], width), jnp.float32)
    for job, (r, s) in enumerate(jobs):

        @pl.when(sources[job])
        def _():
            here = right.at[job]
            pltpu.make_async_copy(here, here, sems.at[job]).wait()
            later = product(r, s, [right[job, t] for t in range(slots)])
            for t in range(slots):
                acc[r, field(r, 0, s * slots + t)] += later[:, t * width : (t + 1) * width]

    for r in range(rows_here):
        for slot in range(slot_total):

            @pl.when((field(r, 2, slot) == (1 if late else 0)) & (field(r, 0, slot) == slot))
            def _():
                finish(r, slot)


def expand_split(q, late, meta, own, inputs, before, width):
    rows_here, slots, side, _ = own.shape
    vmem, anywhere = pl.BlockSpec(memory_space=pltpu.VMEM), pl.BlockSpec(memory_space=pl.ANY)
    jobs = rows_here * (slots - 1)
    acc = jax.ShapeDtypeStruct((rows_here, slots * slots, side, width), jnp.float32)
    outs = [jax.ShapeDtypeStruct(acc.shape, jnp.bfloat16), jax.ShapeDtypeStruct((16, width), jnp.float32)]
    specs = [vmem] * 3 + [anywhere] * (len(inputs) - 3) if late else [anywhere] * len(inputs)
    return pl.pallas_call(
        functools.partial(split_kernel, q, rows_here, slots, late),
        in_specs=[pl.BlockSpec(memory_space=pltpu.SMEM), vmem] + specs + [anywhere],
        out_specs=[vmem] * (2 if late else 3),
        out_shape=outs if late else [acc] + outs,
        scratch_shapes=([pltpu.VMEM(acc.shape, jnp.float32)] if late else [])
        + [pltpu.VMEM((jobs, slots, side, width), jnp.bfloat16), pltpu.SemaphoreType.DMA((jobs,))],
        compiler_params=pltpu.CompilerParams(vmem_limit_bytes=12 * 2**20),
        cost_estimate=pl.CostEstimate(
            flops=rows_here * slots * slots * side * side * width,
            bytes_accessed=8 * 2**20,
            transcendentals=0,
        ),
        name=f"{'late' if late else 'early'}{q}",
    )(meta, own, *inputs, before)


def expand(q, meta, own, beside, across, before):
    rows_here, slots, side, width = across[0].shape
    vmem, anywhere = pl.BlockSpec(memory_space=pltpu.VMEM), pl.BlockSpec(memory_space=pl.ANY)
    jobs = rows_here * (slots - 1)
    return pl.pallas_call(
        functools.partial(expand_kernel, q, rows_here, slots),
        in_specs=[pl.BlockSpec(memory_space=pltpu.SMEM), vmem] + [anywhere] * (len(across) + 2),
        out_specs=[vmem, vmem],
        out_shape=[
            jax.ShapeDtypeStruct((rows_here, slots * slots, side, width), jnp.bfloat16),
            jax.ShapeDtypeStruct((16, width), jnp.float32),
        ],
        scratch_shapes=[
            pltpu.VMEM((rows_here, slots * (slots - 1) + 1, side, width), jnp.float32),
            pltpu.VMEM((jobs, slots, side, width), jnp.bfloat16),
            pltpu.SemaphoreType.DMA((jobs,)),
        ],
        compiler_params=pltpu.CompilerParams(vmem_limit_bytes=24 * 2**20),
        cost_estimate=pl.CostEstimate(
            flops=2 * rows_here * slots * slots * side * side * width,
            bytes_accessed=12 * 2**20,
            transcendentals=0,
        ),
        name=f"expand{q}",
    )(meta, own, beside, *across, before)


def inflate_kernel(scale, slots, first, more, meta, totals, *refs):
    count = len(refs) - 3 - more
    parts, (out, made, sems) = refs[:count], refs[-3:]
    rows_here, slot_total, side, width = parts[0].shape
    depth = made.shape[0]
    cols = pl.ds(first * width, count * width)
    jobs = [(r, slot) for r in range(rows_here) for slot in range(slot_total)]

    def sending(number):
        r, slot = jobs[number]
        at = number % depth
        return pltpu.make_async_copy(made.at[at], out.at[r, slot, :, cols], sems.at[at])

    def leads(number):
        r, slot = jobs[number]
        return meta[r * FIELDS + 2 * slots + slot] == slot

    for number, (r, slot) in enumerate(jobs):
        if number >= depth:

            @pl.when(leads(number - depth))
            def _():
                sending(number - depth).wait()

        @pl.when(leads(number))
        def _():
            place = meta[r * FIELDS + 2 * slots + slots * slots + slot]
            factor = scale / totals[pl.ds(place, 1), :]
            for q, part in enumerate(parts):
                wide = part[r, slot].astype(jnp.float32)
                here = slice(q * width, (q + 1) * width)
                made[number % depth, :, here] = (wide * wide * factor[:, here]).astype(jnp.bfloat16)
            sending(number).start()

    for number in range(len(jobs) - depth, len(jobs)):

        @pl.when(leads(number))
        def _():
            sending(number).wait()


def inflate(scale, slots, meta, totals, parts, first=0, so_far=None):
    rows_here, slot_total, side, width = parts[0].shape
    vmem, anywhere = pl.BlockSpec(memory_space=pltpu.VMEM), pl.BlockSpec(memory_space=pl.ANY)
    more = [] if so_far is None else [so_far]
    return pl.pallas_call(
        functools.partial(inflate_kernel, scale, slots, first, len(more)),
        in_specs=[pl.BlockSpec(memory_space=pltpu.SMEM), vmem] + [vmem] * len(parts) + [anywhere] * len(more),
        out_specs=anywhere,
        out_shape=jax.ShapeDtypeStruct((rows_here, slot_total, side, width * CHUNKS), jnp.bfloat16),
        scratch_shapes=[
            pltpu.VMEM((9, side, width * len(parts)), jnp.bfloat16),
            pltpu.SemaphoreType.DMA((9,)),
        ],
        input_output_aliases={2 + len(parts): 0} if more else {},
        compiler_params=pltpu.CompilerParams(vmem_limit_bytes=12 * 2**20),
        cost_estimate=pl.CostEstimate(flops=2**22 * len(parts), bytes_accessed=4 * 2**20 * len(parts), transcendentals=0),
        name=f"inflate{first}",
    )(meta, totals, *parts, *more)


def blank_kernel(slots, meta, before, out, zero, sem):
    del before
    zero[...] = jnp.zeros_like(zero)
    jobs = [(r, slot) for r in range(out.shape[0]) for slot in range(out.shape[1])]
    for finish in (False, True):
        for number, (r, slot) in enumerate(jobs):

            @pl.when(meta[r * FIELDS + 2 * slots + slot] != slot)
            def _():
                copy = pltpu.make_async_copy(zero, out.at[r, slot], sem.at[number])
                copy.wait() if finish else copy.start()


def blank_slots(meta, before, rows_here, slots, side):
    anywhere = pl.BlockSpec(memory_space=pl.ANY)
    shape = (rows_here, slots * slots, side, side)
    return pl.pallas_call(
        functools.partial(blank_kernel, slots),
        in_specs=[pl.BlockSpec(memory_space=pltpu.SMEM), anywhere],
        out_specs=anywhere,
        out_shape=jax.ShapeDtypeStruct(shape, jnp.bfloat16),
        scratch_shapes=[pltpu.VMEM(shape[2:], jnp.bfloat16), pltpu.SemaphoreType.DMA((shape[0] * shape[1],))],
        compiler_params=pltpu.CompilerParams(vmem_limit_bytes=2 * 2**20),
        cost_estimate=pl.CostEstimate(flops=0, bytes_accessed=2**21, transcendentals=0),
        name="blank",
    )(meta, before)


def columns_kernel(q, width, tiles, *refs):
    out, sem = refs[-2:]
    copy = pltpu.make_async_copy(tiles.at[:, :, :, pl.ds(q * width, width)], out, sem)
    copy.start()
    copy.wait()


def columns_of(tiles, q, width, after):
    anywhere, far = pl.BlockSpec(memory_space=pl.ANY), pl.BlockSpec(memory_space=pltpu.HBM)
    return pl.pallas_call(
        functools.partial(columns_kernel, q, width),
        in_specs=[far] + [anywhere] * len(after),
        out_specs=far,
        out_shape=jax.ShapeDtypeStruct((*tiles.shape[:3], width), tiles.dtype),
        scratch_shapes=[pltpu.SemaphoreType.DMA],
        compiler_params=pltpu.CompilerParams(vmem_limit_bytes=2**20),
        cost_estimate=pl.CostEstimate(flops=0, bytes_accessed=2**20, transcendentals=0),
        name=f"columns{q}",
    )(tiles, *after)


def body(matrix_tiles, pattern):
    rows_here, slots, side, _ = matrix_tiles.shape
    scale = float(slots * slots * side)
    devices = lax.axis_size(AXES)
    assert rows_here == W and lax.axis_size("depth") == 2
    core = lax.axis_index("depth")
    start = lax.axis_index(AXES) * rows_here
    chips = devices // 2
    swap = both_ways([(2 * c, 2 * c + 1) for c in range(chips)])
    next_chip = both_ways([(2 * c + 1, 2 * c + 2) for c in range(chips - 1)])
    second_chip = both_ways([(2 * c + 1, 2 * c + 4) for c in range(chips - 2)])

    width = side // CHUNKS
    here = lax.axis_index(AXES)
    rows, columns = lax.axis_size("row"), lax.axis_size("col")
    beside = lax.ppermute(matrix_tiles, AXES, swap)
    pieces = [matrix_tiles[..., :width]]
    pieces.append(columns_of(matrix_tiles, 1, width, [pieces[0]]))
    pieces.append(columns_of(matrix_tiles, 2, width, [beside, pieces[1]]))
    kind = jnp.int32(0)
    if rows == 4:
        legs, kinds = detours(rows - 1, columns)
        straight = [pair for pair in next_chip if pair[1] not in kinds]
        side_leg = lax.ppermute(columns_of(matrix_tiles, 0, width, [pieces[1]]), AXES, legs[1][0])
        stops = [lax.ppermute(pieces[0], AXES, straight + legs[0][0]), side_leg]
        first = [stops[0]] + [lax.ppermute(stop, AXES, home_leg) for stop, (_, home_leg) in zip(stops, legs)]
        for target, number in kinds.items():
            kind = jnp.where(here == target, number, kind)
        follow = stops
        order = [*range(1, CHUNKS - 1), 0, CHUNKS - 1]
    else:
        first = [lax.ppermute(pieces[0], AXES, next_chip)]
        follow = first
        order = [*range(CHUNKS)]
    across = [first] + [[lax.ppermute(piece, AXES, next_chip)] for piece in pieces[1:]]
    meta = plan(pattern, start, rows_here, core, kind)
    parts, windows = [None] * CHUNKS, [None] * CHUNKS
    before = meta
    halves = {}
    for q in order[:-2]:
        parts[q], windows[q] = expand(q, meta, matrix_tiles, beside, across[q], before)
        before = windows[q]
        if q == order[0]:
            last = columns_of(matrix_tiles, CHUNKS - 1, width, [before, *follow])
            across.append([lax.ppermute(last, AXES, next_chip)])
        if q == order[0]:
            before = so_far = blank_slots(meta, last, rows_here, slots, side)
        split = order[-1] if q == order[0] else order[-2]
        halves[split] = expand_split(split, False, meta, matrix_tiles, [beside], before, width)
        before = halves[split][2]
    for q in order[-2:]:
        parts[q], windows[q] = expand_split(q, True, meta, matrix_tiles, [*halves[q], *across[q]], before, width)
        before = windows[q]
    window = jnp.concatenate(windows, axis=1)

    chip_rows = 2 * rows_here
    used = chip_rows + 4 * W
    window = window[:used]
    chip = window + lax.ppermute(window, AXES, swap)
    low = core == 0
    near, far = 2 * chip_rows, chip_rows
    first = lax.ppermute(jnp.where(low, chip[:near], chip[used - near :]), AXES, next_chip)
    second = lax.ppermute(jnp.where(low, chip[:far], chip[used - far :]), AXES, second_chip)
    blank = jnp.zeros((chip_rows, chip.shape[1]), chip.dtype)
    gathered = first + jnp.where(low, jnp.concatenate([second, blank]), jnp.concatenate([blank, second]))
    other = lax.ppermute(gathered, AXES, swap)
    below, above = jnp.where(low, gathered, other), jnp.where(low, other, gathered)
    totals = chip + jnp.concatenate([below, blank]) + jnp.concatenate([blank, above])
    return inflate(scale, slots, meta, totals, parts, so_far=so_far)


def solution(mesh):
    return jax.shard_map(
        body,
        mesh=mesh,
        in_specs=(P(AXES, None, None, None), P()),
        out_specs=P(AXES, None, None, None),
        check_vma=False,
    )
```

```python
import functools

import jax
import jax.numpy as jnp
from jax import lax
from jax.experimental import pallas as pl
from jax.experimental.pallas import tpu as pltpu
from jax.sharding import PartitionSpec as P

W = 2
AXES = ("row", "col", "depth")
CHUNKS = 4
FIELDS = 33


def both_ways(pairs):
    return pairs + [(b, a) for a, b in pairs]


def plan(pattern, start, rows_here, core, kind):
    row_cols = lax.dynamic_slice_in_dim(pattern, start, rows_here, 0)
    slots = pattern.shape[1]
    out_cols = jnp.take(pattern, row_cols, axis=0).reshape(rows_here, slots * slots)
    offset = row_cols - start
    inside = (offset >= 0) & (offset < rows_here)
    above = offset >= rows_here
    beside = jnp.where(core == 0, above, offset < 0)
    source = jnp.where(inside, 0, jnp.where(beside, 1, 2))
    line = jnp.where(inside, offset, jnp.where(above, offset - rows_here, offset + rows_here))
    positions = jnp.arange(slots * slots, dtype=jnp.int32)
    matched = out_cols[:, :, None] == out_cols[:, None, :]
    lead = jnp.min(jnp.where(matched, positions[None, None, :], slots * slots), axis=2)
    window = out_cols - (start - core * rows_here - 2 * W)
    far = jnp.repeat(source == 2, slots, axis=1)
    touched = jnp.any(far[:, :, None] & (lead[:, :, None] == positions[None, None, :]), axis=1)
    scalars = jnp.concatenate([source, line, lead, window, touched], axis=1).astype(jnp.int32).reshape(-1)
    return jnp.concatenate([scalars, kind.astype(jnp.int32)[None]])


def detours(last_row, columns):
    def device(row, col, core):
        return (row * columns + col) * 2 + core

    top = columns - 1
    spare_up, spare_down = [device(0, 0, 0), device(0, 0, 1)], [device(last_row, top, 1), device(last_row, top, 0)]
    first, second, kinds = [], [], {}
    legs = [(first, []), (second, [])]
    for row in range(last_row):
        low, high = device(row, top, 1), device(row + 1, 0, 0)
        for source, target, spare, turn in ((high, low, spare_up, row), (low, high, spare_down, last_row - 1 - row)):
            which = 0 if turn == last_row - 1 else 1
            stop = spare[turn % 2]
            legs[which][0].append((source, stop))
            legs[which][1].append((stop, target))
            kinds[target] = which + 1
    return legs, kinds


def expand_kernel(q, rows_here, slots, meta, own, *refs):
    out, win, acc, right, sems = refs[-5:]
    beside, across = refs[0], refs[1:-6]
    width = out.shape[3]
    cols = pl.ds(q * width, width)

    def fetch(r, s):
        source, line = meta[r * FIELDS + s], meta[r * FIELDS + slots + s]
        if len(across) > 1:
            source = jnp.where(source == 2, 2 + meta[rows_here * FIELDS], source)
        job = r * (slots - 1) + s - 1
        places = [own.at[line, :, :, cols], beside.at[line, :, :, cols]] + [part.at[line] for part in across]
        for number, place in enumerate(places):

            @pl.when(source == number)
            def _():
                pltpu.make_async_copy(place, right.at[job], sems.at[job]).start()

    for r in range(rows_here):
        for s in range(1, slots):
            fetch(r, s)
    win[...] = jnp.zeros_like(win)

    def product(r, s, tiles):
        return jnp.dot(own[r, s], jnp.concatenate(tiles, axis=1), preferred_element_type=jnp.float32)

    def finish(r, slot, total):
        values = total.astype(jnp.bfloat16)
        out[r, slot] = values
        wide = values.astype(jnp.float32)
        place = meta[r * FIELDS + 2 * slots + slots * slots + slot]
        win[pl.ds(place, 1), :] += jnp.sum(wide * wide, axis=0, keepdims=True)

    for r in range(rows_here):
        first = product(r, 0, [own[r, t, :, cols] for t in range(slots)])
        for t in range(slots):
            acc[r, t] = first[:, t * width : (t + 1) * width]
    for r in range(rows_here):
        for s in range(1, slots):
            job = r * (slots - 1) + s - 1
            pltpu.make_async_copy(across[0].at[0], right.at[job], sems.at[job]).wait()
            later = product(r, s, [right[job, t] for t in range(slots)])
            for t in range(slots):
                part = later[:, t * width : (t + 1) * width]
                slot = s * slots + t
                lead = meta[r * FIELDS + 2 * slots + slot]
                kept = part * jnp.where(lead == slot, 1.0, 0.0)
                acc[r, jnp.where(lead == slot, slots * (slots - 1), lead)] += part
                if s == slots - 1:
                    finish(r, slot, kept)
                else:
                    acc[r, slot] = kept

        for slot in range(slots * (slots - 1)):
            finish(r, slot, acc[r, slot])


def split_kernel(q, rows_here, slots, late, meta, own, *refs):
    slot_total = slots * slots
    width = refs[0].shape[3] if late else refs[2].shape[3]
    cols = pl.ds(q * width, width)
    if late:
        acc_before, out_before, win_before = refs[:3]
        out, win, acc, right, sems = refs[-5:]
        across = refs[3:-6]
    else:
        beside = refs[0]
        acc, out, win, right, sems = refs[-5:]
    sources, lines = {}, {}
    jobs = [(r, s) for r in range(rows_here) for s in range(1, slots)]
    for job, (r, s) in enumerate(jobs):
        source, line = meta[r * FIELDS + s], meta[r * FIELDS + slots + s]
        if late:
            mine = source == 2
            which = meta[rows_here * FIELDS] if len(across) > 1 else 0
            places = [(mine & (which == number), part.at[line]) for number, part in enumerate(across)]
        else:
            mine = source != 2
            places = [(source == 0, own.at[line, :, :, cols]), (source == 1, beside.at[line, :, :, cols])]
        sources[job] = mine
        for chosen, place in places:

            @pl.when(chosen)
            def _():
                pltpu.make_async_copy(place, right.at[job], sems.at[job]).start()

    def field(r, group, slot):
        return meta[r * FIELDS + 2 * slots + group * slot_total + slot]

    def product(r, s, tiles):
        return jnp.dot(own[r, s], jnp.concatenate(tiles, axis=1), preferred_element_type=jnp.float32)

    def finish(r, slot):
        values = acc[r, slot].astype(jnp.bfloat16)
        out[r, slot] = values
        wide = values.astype(jnp.float32)
        win[pl.ds(field(r, 1, slot), 1), :] += jnp.sum(wide * wide, axis=0, keepdims=True)

    if late:
        win[...] = win_before[...]
        for r in range(rows_here):
            for slot in range(slot_total):
                touched = field(r, 2, slot) == 1

                @pl.when(touched)
                def _():
                    acc[r, slot] = acc_before[r, slot]

                @pl.when(jnp.logical_not(touched))
                def _():
                    out[r, slot] = out_before[r, slot]
    else:
        win[...] = jnp.zeros_like(win)
        for r in range(rows_here):
            first = product(r, 0, [own[r, t, :, cols] for t in range(slots)])
            for t in range(slots):
                acc[r, t] = first[:, t * width : (t + 1) * width]
            for slot in range(slots, slot_total):
                acc[r, slot] = jnp.zeros((acc.shape[2], width), jnp.float32)
    for job, (r, s) in enumerate(jobs):

        @pl.when(sources[job])
        def _():
            here = right.at[job]
            pltpu.make_async_copy(here, here, sems.at[job]).wait()
            later = product(r, s, [right[job, t] for t in range(slots)])
            for t in range(slots):
                acc[r, field(r, 0, s * slots + t)] += later[:, t * width : (t + 1) * width]

    for r in range(rows_here):
        for slot in range(slot_total):

            @pl.when(field(r, 2, slot) == (1 if late else 0))
            def _():
                finish(r, slot)


def expand_split(q, late, meta, own, inputs, before, width):
    rows_here, slots, side, _ = own.shape
    vmem, anywhere = pl.BlockSpec(memory_space=pltpu.VMEM), pl.BlockSpec(memory_space=pl.ANY)
    jobs = rows_here * (slots - 1)
    acc = jax.ShapeDtypeStruct((rows_here, slots * slots, side, width), jnp.float32)
    outs = [jax.ShapeDtypeStruct(acc.shape, jnp.bfloat16), jax.ShapeDtypeStruct((16, width), jnp.float32)]
    specs = [vmem] * 3 + [anywhere] * (len(inputs) - 3) if late else [anywhere] * len(inputs)
    return pl.pallas_call(
        functools.partial(split_kernel, q, rows_here, slots, late),
        in_specs=[pl.BlockSpec(memory_space=pltpu.SMEM), vmem] + specs + [anywhere],
        out_specs=[vmem] * (2 if late else 3),
        out_shape=outs if late else [acc] + outs,
        scratch_shapes=([pltpu.VMEM(acc.shape, jnp.float32)] if late else [])
        + [pltpu.VMEM((jobs, slots, side, width), jnp.bfloat16), pltpu.SemaphoreType.DMA((jobs,))],
        compiler_params=pltpu.CompilerParams(vmem_limit_bytes=12 * 2**20),
        cost_estimate=pl.CostEstimate(
            flops=rows_here * slots * slots * side * side * width,
            bytes_accessed=8 * 2**20,
            transcendentals=0,
        ),
        name=f"{'late' if late else 'early'}{q}",
    )(meta, own, *inputs, before)


def expand(q, meta, own, beside, across, before):
    rows_here, slots, side, width = across[0].shape
    vmem, anywhere = pl.BlockSpec(memory_space=pltpu.VMEM), pl.BlockSpec(memory_space=pl.ANY)
    jobs = rows_here * (slots - 1)
    return pl.pallas_call(
        functools.partial(expand_kernel, q, rows_here, slots),
        in_specs=[pl.BlockSpec(memory_space=pltpu.SMEM), vmem] + [anywhere] * (len(across) + 2),
        out_specs=[vmem, vmem],
        out_shape=[
            jax.ShapeDtypeStruct((rows_here, slots * slots, side, width), jnp.bfloat16),
            jax.ShapeDtypeStruct((16, width), jnp.float32),
        ],
        scratch_shapes=[
            pltpu.VMEM((rows_here, slots * (slots - 1) + 1, side, width), jnp.float32),
            pltpu.VMEM((jobs, slots, side, width), jnp.bfloat16),
            pltpu.SemaphoreType.DMA((jobs,)),
        ],
        compiler_params=pltpu.CompilerParams(vmem_limit_bytes=24 * 2**20),
        cost_estimate=pl.CostEstimate(
            flops=2 * rows_here * slots * slots * side * side * width,
            bytes_accessed=12 * 2**20,
            transcendentals=0,
        ),
        name=f"expand{q}",
    )(meta, own, beside, *across, before)


def inflate_kernel(scale, slots, first, more, meta, totals, *refs):
    count = len(refs) - 3 - more
    parts, (out, made, sems) = refs[:count], refs[-3:]
    rows_here, slot_total, side, width = parts[0].shape
    depth = made.shape[0]
    cols = pl.ds(first * width, count * width)
    jobs = [(r, slot) for r in range(rows_here) for slot in range(slot_total)]

    def sending(number):
        r, slot = jobs[number]
        at = number % depth
        return pltpu.make_async_copy(made.at[at], out.at[r, slot, :, cols], sems.at[at])

    def leads(number):
        r, slot = jobs[number]
        return meta[r * FIELDS + 2 * slots + slot] == slot

    for number, (r, slot) in enumerate(jobs):
        if number >= depth:

            @pl.when(leads(number - depth))
            def _():
                sending(number - depth).wait()

        @pl.when(leads(number))
        def _():
            place = meta[r * FIELDS + 2 * slots + slots * slots + slot]
            factor = scale / totals[pl.ds(place, 1), :]
            for q, part in enumerate(parts):
                wide = part[r, slot].astype(jnp.float32)
                here = slice(q * width, (q + 1) * width)
                made[number % depth, :, here] = (wide * wide * factor[:, here]).astype(jnp.bfloat16)
            sending(number).start()

    for number in range(len(jobs) - depth, len(jobs)):

        @pl.when(leads(number))
        def _():
            sending(number).wait()


def inflate(scale, slots, meta, totals, parts, first=0, so_far=None):
    rows_here, slot_total, side, width = parts[0].shape
    vmem, anywhere = pl.BlockSpec(memory_space=pltpu.VMEM), pl.BlockSpec(memory_space=pl.ANY)
    more = [] if so_far is None else [so_far]
    return pl.pallas_call(
        functools.partial(inflate_kernel, scale, slots, first, len(more)),
        in_specs=[pl.BlockSpec(memory_space=pltpu.SMEM), vmem] + [vmem] * len(parts) + [anywhere] * len(more),
        out_specs=anywhere,
        out_shape=jax.ShapeDtypeStruct((rows_here, slot_total, side, width * CHUNKS), jnp.bfloat16),
        scratch_shapes=[
            pltpu.VMEM((12, side, width * len(parts)), jnp.bfloat16),
            pltpu.SemaphoreType.DMA((12,)),
        ],
        input_output_aliases={2 + len(parts): 0} if more else {},
        compiler_params=pltpu.CompilerParams(vmem_limit_bytes=12 * 2**20),
        cost_estimate=pl.CostEstimate(flops=2**22 * len(parts), bytes_accessed=4 * 2**20 * len(parts), transcendentals=0),
        name=f"inflate{first}",
    )(meta, totals, *parts, *more)


def blank_kernel(slots, meta, before, out, zero, sem):
    del before
    zero[...] = jnp.zeros_like(zero)
    jobs = [(r, slot) for r in range(out.shape[0]) for slot in range(out.shape[1])]
    for finish in (False, True):
        for number, (r, slot) in enumerate(jobs):

            @pl.when(meta[r * FIELDS + 2 * slots + slot] != slot)
            def _():
                copy = pltpu.make_async_copy(zero, out.at[r, slot], sem.at[number])
                copy.wait() if finish else copy.start()


def blank_slots(meta, before, rows_here, slots, side):
    anywhere = pl.BlockSpec(memory_space=pl.ANY)
    shape = (rows_here, slots * slots, side, side)
    return pl.pallas_call(
        functools.partial(blank_kernel, slots),
        in_specs=[pl.BlockSpec(memory_space=pltpu.SMEM), anywhere],
        out_specs=anywhere,
        out_shape=jax.ShapeDtypeStruct(shape, jnp.bfloat16),
        scratch_shapes=[pltpu.VMEM(shape[2:], jnp.bfloat16), pltpu.SemaphoreType.DMA((shape[0] * shape[1],))],
        compiler_params=pltpu.CompilerParams(vmem_limit_bytes=2 * 2**20),
        cost_estimate=pl.CostEstimate(flops=0, bytes_accessed=2**21, transcendentals=0),
        name="blank",
    )(meta, before)


def columns_kernel(q, width, tiles, *refs):
    out, sem = refs[-2:]
    copy = pltpu.make_async_copy(tiles.at[:, :, :, pl.ds(q * width, width)], out, sem)
    copy.start()
    copy.wait()


def columns_of(tiles, q, width, after):
    anywhere, far = pl.BlockSpec(memory_space=pl.ANY), pl.BlockSpec(memory_space=pltpu.HBM)
    return pl.pallas_call(
        functools.partial(columns_kernel, q, width),
        in_specs=[far] + [anywhere] * len(after),
        out_specs=far,
        out_shape=jax.ShapeDtypeStruct((*tiles.shape[:3], width), tiles.dtype),
        scratch_shapes=[pltpu.SemaphoreType.DMA],
        compiler_params=pltpu.CompilerParams(vmem_limit_bytes=2**20),
        cost_estimate=pl.CostEstimate(flops=0, bytes_accessed=2**20, transcendentals=0),
        name=f"columns{q}",
    )(tiles, *after)


def body(matrix_tiles, pattern):
    rows_here, slots, side, _ = matrix_tiles.shape
    scale = float(slots * slots * side)
    devices = lax.axis_size(AXES)
    assert rows_here == W and lax.axis_size("depth") == 2
    core = lax.axis_index("depth")
    start = lax.axis_index(AXES) * rows_here
    chips = devices // 2
    swap = both_ways([(2 * c, 2 * c + 1) for c in range(chips)])
    next_chip = both_ways([(2 * c + 1, 2 * c + 2) for c in range(chips - 1)])
    second_chip = both_ways([(2 * c + 1, 2 * c + 4) for c in range(chips - 2)])

    width = side // CHUNKS
    here = lax.axis_index(AXES)
    rows, columns = lax.axis_size("row"), lax.axis_size("col")
    beside = lax.ppermute(matrix_tiles, AXES, swap)
    pieces = [matrix_tiles[..., :width]]
    pieces.append(columns_of(matrix_tiles, 1, width, [pieces[0]]))
    pieces.append(columns_of(matrix_tiles, 2, width, [beside, pieces[1]]))
    kind = jnp.int32(0)
    if rows == 4:
        legs, kinds = detours(rows - 1, columns)
        straight = [pair for pair in next_chip if pair[1] not in kinds]
        side_leg = lax.ppermute(columns_of(matrix_tiles, 0, width, [pieces[1]]), AXES, legs[1][0])
        stops = [lax.ppermute(pieces[0], AXES, straight + legs[0][0]), side_leg]
        first = [stops[0]] + [lax.ppermute(stop, AXES, home_leg) for stop, (_, home_leg) in zip(stops, legs)]
        for target, number in kinds.items():
            kind = jnp.where(here == target, number, kind)
        follow = stops
        order = [*range(1, CHUNKS - 1), 0, CHUNKS - 1]
    else:
        first = [lax.ppermute(pieces[0], AXES, next_chip)]
        follow = first
        order = [*range(CHUNKS)]
    across = [first] + [[lax.ppermute(piece, AXES, next_chip)] for piece in pieces[1:]]
    meta = plan(pattern, start, rows_here, core, kind)
    parts, windows = [None] * CHUNKS, [None] * CHUNKS
    before = meta
    halves = {}
    for q in order[:-2]:
        parts[q], windows[q] = expand(q, meta, matrix_tiles, beside, across[q], before)
        before = windows[q]
        if q == order[0]:
            last = columns_of(matrix_tiles, CHUNKS - 1, width, [before, *follow])
            across.append([lax.ppermute(last, AXES, next_chip)])
        if q == order[0]:
            before = so_far = blank_slots(meta, last, rows_here, slots, side)
        split = order[-1] if q == order[0] else order[-2]
        halves[split] = expand_split(split, False, meta, matrix_tiles, [beside], before, width)
        before = halves[split][2]
    for q in order[-2:]:
        parts[q], windows[q] = expand_split(q, True, meta, matrix_tiles, [*halves[q], *across[q]], before, width)
        before = windows[q]
    window = jnp.concatenate(windows, axis=1)

    chip_rows = 2 * rows_here
    used = chip_rows + 4 * W
    window = window[:used]
    chip = window + lax.ppermute(window, AXES, swap)
    low = core == 0
    near, far = 2 * chip_rows, chip_rows
    first = lax.ppermute(jnp.where(low, chip[:near], chip[used - near :]), AXES, next_chip)
    second = lax.ppermute(jnp.where(low, chip[:far], chip[used - far :]), AXES, second_chip)
    blank = jnp.zeros((chip_rows, chip.shape[1]), chip.dtype)
    gathered = first + jnp.where(low, jnp.concatenate([second, blank]), jnp.concatenate([blank, second]))
    other = lax.ppermute(gathered, AXES, swap)
    below, above = jnp.where(low, gathered, other), jnp.where(low, other, gathered)
    totals = chip + jnp.concatenate([below, blank]) + jnp.concatenate([blank, above])
    return inflate(scale, slots, meta, totals, parts, so_far=so_far)


def solution(mesh):
    return jax.shard_map(
        body,
        mesh=mesh,
        in_specs=(P(AXES, None, None, None), P()),
        out_specs=P(AXES, None, None, None),
        check_vma=False,
    )
```
